256 devices in a mesh: ctx: 64 (over y, x, z_hi, core), grp: 4 (over z_lo).
Axes of the slice: x: 4, y: 4, z: 8 (z_hi: 2, z_lo: 4; z = z_hi * 4 + z_lo), core: 2. Of those that a mesh axis runs over, the one named last changes fastest.
Arguments:
- query_in: float32 [1024, 16384], P('grp', 'ctx'), may hold values from -6 to 6
- key_in: float32 [1024, 16384], P('grp', 'ctx'), may hold values from -6 to 6
- value_in: float32 [1024, 16384], P('grp', 'ctx'), may hold values from -6 to 6
- short_weight: float32 [3, 7, 1024], P(None, None, 'grp'), may hold values from -2 to 2
- long_filter: float32 [1024, 16384], P('grp', 'ctx'), may hold values from -1.1 to 1.1
- skip_weight: float32 [1024], P('grp'), may hold values from -4 to 4
Outputs:
- mixed: float32 [1024, 16384], P('grp', 'ctx')
The draws below stay inside these ranges and needn't reach their ends.
All inputs are finite; a program needn't handle non-finite values.
Results may differ from the reference program's by a relative error of at most 0.00012.
Values sent between devices are 32-bit elements; how exact they have to be, the bound alone decides.
No kernel may reach another device: no remote copies, remote signals or barrier semaphores. Data moves between devices by JAX's collectives and lax.ppermute only.
A program may use at most 64 MiB of HBM per device.

```python
import math
import jax
import jax.numpy as jnp
from jax import lax

D = 1024
TAPS = 7
SEQ = 16384


def draw_long_filter(key, part):
    first_key, second_key = jax.random.split(key)
    decay = jnp.exp(jax.random.uniform(first_key, (D, 1), jnp.float32, math.log(30.0), math.log(2.0 * SEQ)))
    lagged = jnp.arange(SEQ, dtype=jnp.float32)[None, :]
    envelope = jnp.exp(-lagged / decay)
    factor = jnp.sqrt(2.0 / decay) / jnp.sqrt(1.0 - jnp.exp(-2.0 * SEQ / decay))
    noise = jax.random.truncated_normal(second_key, -4.0, 4.0, (D, SEQ), jnp.float32)
    result = noise * envelope * factor
    return result.astype(jnp.float32)


def levels(rng, extent, shards, least, top_value):
    loudness = 1.0
    for dim, parts in shards:
        heights = jax.random.uniform(jax.random.fold_in(jax.random.fold_in(rng, 6), dim), (parts,), jnp.float32, least / len(shards), top_value / len(shards))
        loudness = loudness * jnp.repeat(jnp.exp(heights), extent[dim] // parts).reshape((-1,) + (1,) * (len(extent) - 1 - dim))
    return loudness


def bell_draw(stream_key, extent, scale, limit, shards=(), kind=jnp.bfloat16):
    values = jax.random.normal(stream_key, extent, jnp.float32) * scale
    if len(shards) > 0:
        values = levels(stream_key, extent, shards, -0.22, 0.18) * values
    return jnp.clip(values, min=-limit, max=limit).astype(kind)


def setup_inputs(seed: int = 0) -> dict:
    splits = jax.random.split(jax.random.key(seed), 7)
    query_in = bell_draw(splits[0], (D, SEQ), 1.0, 6.0, ((0, 4), (1, 64)), jnp.float32)
    key_in = bell_draw(splits[1], (D, SEQ), 1.0, 6.0, ((0, 4), (1, 64)), jnp.float32)
    value_in = bell_draw(splits[2], (D, SEQ), 1.0, 6.0, ((0, 4), (1, 64)), jnp.float32)
    short_weight = bell_draw(splits[3], (3, TAPS, D), TAPS ** -0.5, 2.0, ((2, 4),), jnp.float32)
    long_filter = draw_long_filter(jax.random.fold_in(splits[6], 71), 0)
    skip_weight = bell_draw(splits[5], (D,), 1.0, 4.0, ((0, 4),), jnp.float32)
    return dict(query_in=query_in, key_in=key_in, value_in=value_in, short_weight=short_weight, long_filter=long_filter, skip_weight=skip_weight)


def causal_taps(stream, weights):
    seq_len = stream.shape[1]
    rim_width = weights.shape[0] - 1
    padded = jnp.pad(stream, ((0, 0), (rim_width, 0)))
    total = weights[0][:, None] * padded[:, rim_width:rim_width + seq_len]
    for offset in range(1, weights.shape[0]):
        total = total + weights[offset][:, None] * padded[:, rim_width - offset:rim_width - offset + seq_len]
    return total


def long_block(pair):
    signal, taps_block = pair
    padded_len = 2 * SEQ
    spectrum = jnp.fft.rfft(signal, n=padded_len, axis=1) * jnp.fft.rfft(taps_block, n=padded_len, axis=1)
    return jnp.fft.irfft(spectrum, n=padded_len, axis=1)[:, :SEQ]


def reference(query_in, key_in, value_in, short_weight, long_filter, skip_weight):
    query = causal_taps(query_in, short_weight[0])
    keyed = causal_taps(key_in, short_weight[1])
    valued = causal_taps(value_in, short_weight[2])
    gated = keyed * valued
    block_size = min(64, D)
    conv = lax.map(long_block, (gated.reshape(D // block_size, block_size, SEQ), long_filter.reshape(D // block_size, block_size, SEQ)))
    conv = conv.reshape(D, SEQ)
    return query * (conv + skip_weight[:, None] * gated)
```

```python
import math

import jax
import jax.numpy as jnp
import ml_dtypes
import numpy as np
from jax import lax
from jax.experimental import pallas as pl
from jax.experimental.pallas import tpu as pltpu
from jax.sharding import PartitionSpec as P

LANES = 128
F32 = jnp.float32
BF16 = jnp.bfloat16
VMEM = pl.BlockSpec(memory_space=pltpu.VMEM)
SMEM = pl.BlockSpec(memory_space=pltpu.SMEM)


def halves(table):
    high = table.astype(ml_dtypes.bfloat16)
    low = (table - high.astype(np.float64)).astype(ml_dtypes.bfloat16)
    return high, low


def split(x):
    high = x.astype(BF16)
    return high, (x - high.astype(F32)).astype(BF16)


def tables(blocks, width):
    odd = 2 * np.arange(blocks) + 1
    angle = 2.0 * math.pi * (odd[:, None] * np.arange(blocks)[None, :] % (4 * blocks)) / (4 * blocks)
    high, low = halves(np.concatenate([np.cos(angle), np.sin(angle)], axis=0))
    rows_in = np.concatenate([high, high, low], axis=1)
    scale = 1.0 / (blocks * width)
    high, low = halves(np.concatenate([np.cos(angle), np.sin(angle)], axis=0).T * scale)
    rows_out = np.concatenate([high, high, low], axis=1)
    order = 4 * blocks * width
    turn = 2.0 * math.pi * (odd[:, None] * np.arange(width)[None, :] % order) / order
    index = np.arange(width)
    phase = 2.0 * math.pi * (index[:, None] * index[None, :] % width) / width
    high, low = halves(np.stack([np.cos(phase), np.sin(phase), -np.sin(phase)]))
    return (
        rows_in,
        rows_out,
        np.stack([np.cos(turn), np.sin(turn)]).astype(np.float32),
        high,
        low,
    )


def tap_columns(weights):
    taps, channels = weights.shape
    padded = jnp.concatenate([weights, jnp.zeros((LANES - taps, channels), F32)], axis=0)
    return padded.T


def taps_of_rows(left, right, columns, taps):
    lane = lax.broadcasted_iota(jnp.int32, left.shape, 1)
    weight = columns[:, 0:1]
    first, second = weight * left, weight * right
    spill = jnp.zeros_like(left)
    for j in range(1, taps):
        weight = columns[:, j : j + 1]
        moved_left = weight * pltpu.roll(left, j, 1)
        moved_right = weight * pltpu.roll(right, j, 1)
        head = lane < j
        first = first + jnp.where(head, 0.0, moved_left)
        second = second + jnp.where(head, moved_left, moved_right)
        spill = spill + jnp.where(head, moved_right, 0.0)
    return first, second, spill


def pack_kernel(key_ref, value_ref, filter_ref, weight_ref, out_ref, cols, product, extra, taken):
    taps = weight_ref.shape[1]
    rim = taps - 1
    channels = key_ref.shape[0]
    shards = out_ref.shape[0] // 17
    per = channels // shards
    for h in range(2):
        taken[h] = filter_ref[:, h * LANES : (h + 1) * LANES]
    for c in range(per):
        for h in range(2):
            out_ref[pl.ds(8 + h * 4 + c, shards, stride=17), :] = taken[
                h, pl.ds(c, shards, stride=per), :
            ]
    cols[0] = tap_columns(weight_ref[1])
    cols[1] = tap_columns(weight_ref[2])

    def body(m, carry):
        rows = pl.ds(pl.multiple_of(m * 8, 8), 8)
        k_first, k_second, k_spill = taps_of_rows(
            key_ref[rows, :LANES], key_ref[rows, LANES:], cols[0, rows, :], taps
        )
        v_first, v_second, v_spill = taps_of_rows(
            value_ref[rows, :LANES], value_ref[rows, LANES:], cols[1, rows, :], taps
        )
        lane = lax.broadcasted_iota(jnp.int32, k_first.shape, 1)
        product[0, rows, :] = jnp.where(lane < rim, k_first, k_first * v_first)
        product[1, rows, :] = k_second * v_second
        extra[rows, :] = (
            jnp.where(lane < rim, v_first, 0.0)
            + pltpu.roll(k_spill, rim, 1)
            + pltpu.roll(v_spill, 2 * rim, 1)
        )
        return carry

    lax.fori_loop(0, channels // 8, body, 0, unroll=4)
    line = extra[pl.ds(0, shards, stride=per), :]
    for c in range(1, per):
        line = line + pltpu.roll(extra[pl.ds(c, shards, stride=per), :], 32 * c, 1)
    out_ref[pl.ds(16, shards, stride=17), :] = line
    for c in range(per):
        for h in range(2):
            out_ref[pl.ds(h * 4 + c, shards, stride=17), :] = product[
                h, pl.ds(c, shards, stride=per), :
            ]


def query_kernel(query_ref, weight_ref, out_ref, spill_ref, cols, spilled):
    taps = weight_ref.shape[1]
    channels = query_ref.shape[0]
    cols[...] = tap_columns(weight_ref[0])

    def body(m, carry):
        rows = pl.ds(pl.multiple_of(m * 8, 8), 8)
        first, second, spill = taps_of_rows(
            query_ref[rows, :LANES], query_ref[rows, LANES:], cols[rows, :], taps
        )
        out_ref[rows, :LANES] = first
        out_ref[rows, LANES:] = second
        spilled[rows, :] = spill
        return carry

    lax.fori_loop(0, channels // 8, body, 0, unroll=4)
    spill_ref[...] = spilled[...].T[:8]


def conv_kernel(
    skip_ref, in_ref, rows_in, rows_out, turn, dft_high, dft_low, out_ref, zh, zl, gated, spec
):
    shards = in_ref.shape[0] // 17
    per = skip_ref.shape[0]
    rim = 6
    width = 2 * LANES
    lane = lax.broadcasted_iota(jnp.int32, (shards, LANES), 1)
    block = lax.broadcasted_iota(jnp.int32, (shards, LANES), 0)
    line = in_ref[pl.ds(16, shards, stride=17), :]
    prior = jnp.where(block == 0, 0.0, pltpu.roll(line, 1, 0))
    for c in range(per):
        here = pltpu.roll(line, (LANES - 32 * c) % LANES, 1) if c else line
        key_spill = pltpu.roll(prior, LANES - 32 * c - rim, 1)
        value_spill = pltpu.roll(prior, LANES - 32 * c - 2 * rim, 1)
        first = in_ref[pl.ds(c, shards, stride=17), :]
        first = jnp.where(lane < rim, (first + key_spill) * (here + value_spill), first)
        gated[c] = jnp.concatenate([first, in_ref[pl.ds(4 + c, shards, stride=17), :]], axis=1)
        taken = jnp.concatenate(
            [in_ref[pl.ds(8 + h * 4 + c, shards, stride=17), :] for h in range(2)], axis=1
        )
        for a, signal in enumerate((gated[c], taken)):
            high, low = split(signal)
            both = jnp.dot(
                rows_in[...],
                jnp.concatenate([high, low, high], axis=0),
                preferred_element_type=F32,
            )
            cos_part, sin_part = both[:shards], both[shards:]
            rows = pl.ds((a * per + c) * shards, shards)
            high, low = split(cos_part * turn[0] - sin_part * turn[1])
            zh[0, rows, :] = high
            zl[0, rows, :] = low
            high, low = split(cos_part * turn[1] + sin_part * turn[0])
            zh[1, rows, :] = high
            zl[1, rows, :] = low

    def times(lhs_high, lhs_low, which):
        return (
            jnp.dot(lhs_high, dft_high[which], preferred_element_type=F32)
            + jnp.dot(lhs_low, dft_high[which], preferred_element_type=F32)
            + jnp.dot(lhs_high, dft_low[which], preferred_element_type=F32)
        )

    spec[0] = times(zh[0], zl[0], 0) + times(zh[1], zl[1], 2)
    spec[1] = times(zh[0], zl[0], 1) + times(zh[1], zl[1], 0)
    count = per * shards
    sig_r, sig_i = spec[0, :count], spec[1, :count]
    fil_r, fil_i = spec[0, count:], spec[1, count:]
    real_high, real_low = split(sig_r * fil_r - sig_i * fil_i)
    imag_high, imag_low = split(sig_r * fil_i + sig_i * fil_r)
    back_r = times(real_high, real_low, 0) + times(imag_high, imag_low, 1)
    back_i = times(imag_high, imag_low, 0) + times(real_high, real_low, 2)
    spec[0, :count] = back_r
    spec[1, :count] = back_i
    for c in range(per):
        rows = pl.ds(c * shards, shards)
        br, bi = spec[0, rows, :], spec[1, rows, :]
        high, low = split(
            jnp.concatenate([br * turn[0] + bi * turn[1], bi * turn[0] - br * turn[1]], axis=0)
        )
        result = jnp.dot(
            rows_out[...], jnp.concatenate([high, low, high], axis=0), preferred_element_type=F32
        )
        result = result + skip_ref[c] * gated[c]
        for h in range(2):
            out_ref[pl.ds(h * 4 + c, shards, stride=8), :] = result[:, h * LANES : (h + 1) * LANES]


def gate_kernel(query_ref, spill_ref, conv_ref, out_ref):
    channels = query_ref.shape[0]
    padded = jnp.concatenate([spill_ref[...], jnp.zeros((LANES - 8, channels), F32)], axis=0)
    spill = padded.T
    for m in range(channels // 8):
        rows = slice(m * 8, m * 8 + 8)
        one, two = conv_ref[m * 16 : m * 16 + 8, :], conv_ref[m * 16 + 8 : m * 16 + 16, :]
        left = jnp.concatenate([one[:4], two[:4]], axis=0)
        right = jnp.concatenate([one[4:], two[4:]], axis=0)
        out_ref[rows, :LANES] = (query_ref[rows, :LANES] + spill[rows]) * left
        out_ref[rows, LANES:] = query_ref[rows, LANES:] * right


def on_device(query_in, key_in, value_in, short_weight, long_filter, skip_weight):
    channels, width = query_in.shape
    shards = lax.axis_size("ctx")
    per = channels // shards
    packed = pl.pallas_call(
        pack_kernel,
        out_shape=jax.ShapeDtypeStruct((shards * 17, LANES), F32),
        in_specs=[VMEM] * 4,
        out_specs=VMEM,
        scratch_shapes=[
            pltpu.VMEM((2, channels, LANES), F32),
            pltpu.VMEM((2, channels, LANES), F32),
            pltpu.VMEM((channels, LANES), F32),
            pltpu.VMEM((2, channels, LANES), F32),
        ],
        name="pack",
    )(key_in, value_in, long_filter, short_weight)
    moved = lax.all_to_all(
        packed.reshape(shards, 1, 17 * LANES), "ctx", split_axis=0, concat_axis=0, tiled=True
    ).reshape(shards * 17, LANES)
    query, spill = pl.pallas_call(
        query_kernel,
        out_shape=(
            jax.ShapeDtypeStruct((channels, width), F32),
            jax.ShapeDtypeStruct((8, channels), F32),
        ),
        in_specs=[VMEM] * 2,
        out_specs=(VMEM, VMEM),
        scratch_shapes=[pltpu.VMEM((channels, LANES), F32), pltpu.VMEM((channels, LANES), F32)],
        name="query",
    )(query_in, short_weight)
    spill = lax.ppermute(spill, "ctx", [(i, i + 1) for i in range(shards - 1)])
    skip = lax.dynamic_slice(skip_weight, (lax.axis_index("ctx") * per,), (per,))
    constants = [jnp.asarray(t) for t in tables(shards, width)]
    convolved = pl.pallas_call(
        conv_kernel,
        out_shape=jax.ShapeDtypeStruct((shards * 8, LANES), F32),
        in_specs=[SMEM] + [VMEM] * 6,
        out_specs=VMEM,
        scratch_shapes=[
            pltpu.VMEM((2, 2 * channels, width), BF16),
            pltpu.VMEM((2, 2 * channels, width), BF16),
            pltpu.VMEM((per, shards, width), F32),
            pltpu.VMEM((2, 2 * channels, width), F32),
        ],
        compiler_params=pltpu.CompilerParams(vmem_limit_bytes=24 * 1024 * 1024),
        name="conv",
    )(skip, moved, *constants)
    returned = lax.all_to_all(
        convolved.reshape(shards, 8, LANES), "ctx", split_axis=0, concat_axis=0, tiled=True
    ).reshape(shards * 8, LANES)
    return pl.pallas_call(
        gate_kernel,
        out_shape=jax.ShapeDtypeStruct((channels, width), F32),
        in_specs=[VMEM] * 3,
        out_specs=VMEM,
        name="gate",
    )(query, spill, returned)


def solution(mesh):
    return jax.shard_map(
        on_device,
        mesh=mesh,
        in_specs=(
            P("grp", "ctx"),
            P("grp", "ctx"),
            P("grp", "ctx"),
            P(None, None, "grp"),
            P("grp", "ctx"),
            P("grp"),
        ),
        out_specs=P("grp", "ctx"),
        check_vma=False,
    )
```

```python
import math

import jax
import jax.numpy as jnp
import ml_dtypes
import numpy as np
from jax import lax
from jax.experimental import pallas as pl
from jax.experimental.pallas import tpu as pltpu
from jax.sharding import PartitionSpec as P

LANES = 128
F32 = jnp.float32
BF16 = jnp.bfloat16
VMEM = pl.BlockSpec(memory_space=pltpu.VMEM)
SMEM = pl.BlockSpec(memory_space=pltpu.SMEM)


def halves(table):
    high = table.astype(ml_dtypes.bfloat16)
    low = (table - high.astype(np.float64)).astype(ml_dtypes.bfloat16)
    return high, low


def split(x):
    high = x.astype(BF16)
    return high, (x - high.astype(F32)).astype(BF16)


def tables(blocks, width):
    odd = 2 * np.arange(blocks) + 1
    angle = 2.0 * math.pi * (odd[:, None] * np.arange(blocks)[None, :] % (4 * blocks)) / (4 * blocks)
    high, low = halves(np.concatenate([np.cos(angle), np.sin(angle)], axis=0))
    rows_in = np.concatenate([high, high, low], axis=1)
    scale = 1.0 / (blocks * width)
    high, low = halves(np.concatenate([np.cos(angle), np.sin(angle)], axis=0).T * scale)
    rows_out = np.concatenate([high, high, low], axis=1)
    order = 4 * blocks * width
    turn = 2.0 * math.pi * (odd[:, None] * np.arange(width)[None, :] % order) / order
    index = np.arange(width)
    phase = 2.0 * math.pi * (index[:, None] * index[None, :] % width) / width
    high, low = halves(np.stack([np.cos(phase), np.sin(phase), -np.sin(phase)]))
    return (
        rows_in,
        rows_out,
        np.stack([np.cos(turn), np.sin(turn)]).astype(np.float32),
        high,
        low,
    )


def causal_taps_at(rows_ref, weight_ref, stream, half, start):
    lanes = slice(half * LANES, (half + 1) * LANES)
    total = weight_ref[stream, 0:1, lanes] * rows_ref[half, 8 + start : 16 + start, :]
    for j in range(1, weight_ref.shape[1]):
        moved = rows_ref[half, 8 + start - j : 16 + start - j, :]
        total = total + weight_ref[stream, j : j + 1, lanes] * moved
    return total


def pack_kernel(
    key_ref, value_ref, filter_ref, weight_ref, out_ref, key_rows, value_rows, product, extra, taken
):
    rim = weight_ref.shape[1] - 1
    channels, width = key_ref.shape
    shards = out_ref.shape[0] // 17
    per = channels // shards
    for h in range(2):
        taken[h] = filter_ref[:, h * LANES : (h + 1) * LANES]
    for c in range(per):
        for h in range(2):
            out_ref[pl.ds(8 + h * 4 + c, shards, stride=17), :] = taken[
                h, pl.ds(c, shards, stride=per), :
            ]
    edge = jnp.zeros((8, LANES), F32)
    row = lax.broadcasted_iota(jnp.int32, (8, LANES), 0)
    for half in range(2):
        mine = slice(half * LANES, (half + 1) * LANES)
        for rows, source in ((key_rows, key_ref), (value_rows, value_ref)):
            rows[half, :8, :] = edge
            rows[half, 8 + width :, :] = edge
            for h in range(2):
                part = slice(h * LANES, (h + 1) * LANES)
                rows[half, 8 + h * LANES : 8 + (h + 1) * LANES, :] = source[mine, part].T
        for h in range(2):
            parts = []
            for t in range(h * LANES, (h + 1) * LANES, 8):
                key = causal_taps_at(key_rows, weight_ref, 1, half, t)
                value = causal_taps_at(value_rows, weight_ref, 2, half, t)
                if t == 0:
                    value_head = value
                    parts.append(jnp.where(row < rim, key, key * value))
                else:
                    parts.append(key * value)
            product[h, mine, :] = jnp.concatenate(parts, axis=0).T
        key_spill = causal_taps_at(key_rows, weight_ref, 1, half, width)
        value_spill = causal_taps_at(value_rows, weight_ref, 2, half, width)
        ends = jnp.concatenate(
            [value_head, key_spill, value_spill, jnp.zeros((LANES - 24, LANES), F32)], axis=0
        )
        extra[mine, :] = ends.T
    line = extra[pl.ds(0, shards, stride=per), :]
    for c in range(1, per):
        line = line + pltpu.roll(extra[pl.ds(c, shards, stride=per), :], 32 * c, 1)
    out_ref[pl.ds(16, shards, stride=17), :] = line
    for c in range(per):
        for h in range(2):
            out_ref[pl.ds(h * 4 + c, shards, stride=17), :] = product[
                h, pl.ds(c, shards, stride=per), :
            ]


def query_kernel(query_ref, rim_ref, weight_ref, out_ref, query_rows):
    rim = rim_ref.shape[0]
    width = query_ref.shape[1]
    for half in range(2):
        mine = slice(half * LANES, (half + 1) * LANES)
        query_rows[half, 8 - rim : 8, :] = rim_ref[:, mine]
        for h in range(2):
            part = slice(h * LANES, (h + 1) * LANES)
            query_rows[half, 8 + h * LANES : 8 + (h + 1) * LANES, :] = query_ref[mine, part].T
        for h in range(2):
            parts = [
                causal_taps_at(query_rows, weight_ref, 0, half, t)
                for t in range(h * LANES, (h + 1) * LANES, 8)
            ]
            out_ref[mine, h * LANES : (h + 1) * LANES] = jnp.concatenate(parts, axis=0).T


def conv_kernel(
    skip_ref, in_ref, rows_in, rows_out, turn, dft_high, dft_low, out_ref, zh, zl, gated, spec
):
    shards = in_ref.shape[0] // 17
    per = skip_ref.shape[0]
    rim = 6
    width = 2 * LANES
    lane = lax.broadcasted_iota(jnp.int32, (shards, LANES), 1)
    block = lax.broadcasted_iota(jnp.int32, (shards, LANES), 0)
    line = in_ref[pl.ds(16, shards, stride=17), :]
    prior = jnp.where(block == 0, 0.0, pltpu.roll(line, 1, 0))
    for c in range(per):
        here = pltpu.roll(line, (LANES - 32 * c) % LANES, 1) if c else line
        key_spill = pltpu.roll(prior, LANES - 32 * c - 8, 1)
        value_spill = pltpu.roll(prior, LANES - 32 * c - 16, 1)
        first = in_ref[pl.ds(c, shards, stride=17), :]
        first = jnp.where(lane < rim, (first + key_spill) * (here + value_spill), first)
        gated[c] = jnp.concatenate([first, in_ref[pl.ds(4 + c, shards, stride=17), :]], axis=1)
        taken = jnp.concatenate(
            [in_ref[pl.ds(8 + h * 4 + c, shards, stride=17), :] for h in range(2)], axis=1
        )
        for a, signal in enumerate((gated[c], taken)):
            high, low = split(signal)
            both = jnp.dot(
                rows_in[...],
                jnp.concatenate([high, low, high], axis=0),
                preferred_element_type=F32,
            )
            cos_part, sin_part = both[:shards], both[shards:]
            rows = pl.ds((a * per + c) * shards, shards)
            high, low = split(cos_part * turn[0] - sin_part * turn[1])
            zh[0, rows, :] = high
            zl[0, rows, :] = low
            high, low = split(cos_part * turn[1] + sin_part * turn[0])
            zh[1, rows, :] = high
            zl[1, rows, :] = low

    def times(lhs_high, lhs_low, which):
        return (
            jnp.dot(lhs_high, dft_high[which], preferred_element_type=F32)
            + jnp.dot(lhs_low, dft_high[which], preferred_element_type=F32)
            + jnp.dot(lhs_high, dft_low[which], preferred_element_type=F32)
        )

    spec[0] = times(zh[0], zl[0], 0) + times(zh[1], zl[1], 2)
    spec[1] = times(zh[0], zl[0], 1) + times(zh[1], zl[1], 0)
    count = per * shards
    sig_r, sig_i = spec[0, :count], spec[1, :count]
    fil_r, fil_i = spec[0, count:], spec[1, count:]
    real_high, real_low = split(sig_r * fil_r - sig_i * fil_i)
    imag_high, imag_low = split(sig_r * fil_i + sig_i * fil_r)
    back_r = times(real_high, real_low, 0) + times(imag_high, imag_low, 1)
    back_i = times(imag_high, imag_low, 0) + times(real_high, real_low, 2)
    spec[0, :count] = back_r
    spec[1, :count] = back_i
    for c in range(per):
        rows = pl.ds(c * shards, shards)
        br, bi = spec[0, rows, :], spec[1, rows, :]
        high, low = split(
            jnp.concatenate([br * turn[0] + bi * turn[1], bi * turn[0] - br * turn[1]], axis=0)
        )
        result = jnp.dot(
            rows_out[...], jnp.concatenate([high, low, high], axis=0), preferred_element_type=F32
        )
        result = result + skip_ref[c] * gated[c]
        for h in range(2):
            out_ref[pl.ds(h * 4 + c, shards, stride=8), :] = result[:, h * LANES : (h + 1) * LANES]


def gate_kernel(query_ref, conv_ref, out_ref):
    for m in range(query_ref.shape[0] // 8):
        rows = slice(m * 8, m * 8 + 8)
        one, two = conv_ref[m * 16 : m * 16 + 8, :], conv_ref[m * 16 + 8 : m * 16 + 16, :]
        left = jnp.concatenate([one[:4], two[:4]], axis=0)
        right = jnp.concatenate([one[4:], two[4:]], axis=0)
        out_ref[rows, :LANES] = query_ref[rows, :LANES] * left
        out_ref[rows, LANES:] = query_ref[rows, LANES:] * right


def limit(mebibytes):
    return pltpu.CompilerParams(vmem_limit_bytes=mebibytes * 1024 * 1024)


def on_device(query_in, key_in, value_in, short_weight, long_filter, skip_weight):
    channels, width = query_in.shape
    rim = short_weight.shape[1] - 1
    shards = lax.axis_size("ctx")
    per = channels // shards
    rows = pltpu.VMEM((2, width + 16, LANES), F32)
    packed = pl.pallas_call(
        pack_kernel,
        out_shape=jax.ShapeDtypeStruct((shards * 17, LANES), F32),
        in_specs=[VMEM] * 4,
        out_specs=VMEM,
        scratch_shapes=[
            rows,
            rows,
            pltpu.VMEM((2, channels, LANES), F32),
            pltpu.VMEM((channels, LANES), F32),
            pltpu.VMEM((2, channels, LANES), F32),
        ],
        compiler_params=limit(8),
        name="pack",
    )(key_in, value_in, long_filter, short_weight)
    packed, query_in, short_weight = lax.optimization_barrier((packed, query_in, short_weight))
    moved = lax.all_to_all(
        packed.reshape(shards, 1, 17 * LANES), "ctx", split_axis=0, concat_axis=0, tiled=True
    ).reshape(shards * 17, LANES)
    before = lax.ppermute(
        query_in[:, width - rim :].T, "ctx", [(i, i + 1) for i in range(shards - 1)]
    )
    query = pl.pallas_call(
        query_kernel,
        out_shape=jax.ShapeDtypeStruct((channels, width), F32),
        in_specs=[VMEM] * 3,
        out_specs=VMEM,
        scratch_shapes=[rows],
        compiler_params=limit(8),
        name="query",
    )(query_in, before, short_weight)
    skip = lax.dynamic_slice(skip_weight, (lax.axis_index("ctx") * per,), (per,))
    moved, query = lax.optimization_barrier((moved, query))
    constants = [jnp.asarray(t) for t in tables(shards, width)]
    convolved = pl.pallas_call(
        conv_kernel,
        out_shape=jax.ShapeDtypeStruct((shards * 8, LANES), F32),
        in_specs=[SMEM] + [VMEM] * 6,
        out_specs=VMEM,
        scratch_shapes=[
            pltpu.VMEM((2, 2 * channels, width), BF16),
            pltpu.VMEM((2, 2 * channels, width), BF16),
            pltpu.VMEM((per, shards, width), F32),
            pltpu.VMEM((2, 2 * channels, width), F32),
        ],
        compiler_params=limit(16),
        name="conv",
    )(skip, moved, *constants)
    returned = lax.all_to_all(
        convolved.reshape(shards, 8, LANES), "ctx", split_axis=0, concat_axis=0, tiled=True
    ).reshape(shards * 8, LANES)
    return pl.pallas_call(
        gate_kernel,
        out_shape=jax.ShapeDtypeStruct((channels, width), F32),
        in_specs=[VMEM] * 2,
        out_specs=VMEM,
        compiler_params=limit(8),
        name="gate",
    )(query, returned)


def solution(mesh):
    return jax.shard_map(
        on_device,
        mesh=mesh,
        in_specs=(
            P("grp", "ctx"),
            P("grp", "ctx"),
            P("grp", "ctx"),
            P(None, None, "grp"),
            P("grp", "ctx"),
            P("grp"),
        ),
        out_specs=P("grp", "ctx"),
        check_vma=False,
    )
```

```python
import math

import jax
import jax.numpy as jnp
import ml_dtypes
import numpy as np
from jax import lax
from jax.experimental import pallas as pl
from jax.experimental.pallas import tpu as pltpu
from jax.sharding import PartitionSpec as P

LANES = 128
F32 = jnp.float32
BF16 = jnp.bfloat16
VMEM = pl.BlockSpec(memory_space=pltpu.VMEM)
HBM = pl.BlockSpec(memory_space=pltpu.HBM)
SMEM = pl.BlockSpec(memory_space=pltpu.SMEM)


def halves(table):
    high = table.astype(ml_dtypes.bfloat16)
    low = (table - high.astype(np.float64)).astype(ml_dtypes.bfloat16)
    return high, low


def split(x):
    high = x.astype(BF16)
    return high, (x - high.astype(F32)).astype(BF16)


def tables(blocks, width):
    odd = 2 * np.arange(blocks) + 1
    angle = 2.0 * math.pi * (odd[:, None] * np.arange(blocks)[None, :] % (4 * blocks)) / (4 * blocks)
    high, low = halves(np.concatenate([np.cos(angle), np.sin(angle)], axis=0))
    rows_in = np.concatenate([high, high, low], axis=1)
    scale = 1.0 / (blocks * width)
    high, low = halves(np.concatenate([np.cos(angle), np.sin(angle)], axis=0).T * scale)
    rows_out = np.concatenate([high, high, low], axis=1)
    order = 4 * blocks * width
    turn = 2.0 * math.pi * (odd[:, None] * np.arange(width)[None, :] % order) / order
    index = np.arange(width)
    phase = 2.0 * math.pi * (index[:, None] * index[None, :] % width) / width
    high, low = halves(np.stack([np.cos(phase), np.sin(phase), -np.sin(phase)]))
    return (
        rows_in,
        rows_out,
        np.stack([np.cos(turn), np.sin(turn)]).astype(np.float32),
        high,
        low,
    )


def causal_taps_at(rows_ref, weight_ref, stream, half, start):
    lanes = slice(half * LANES, (half + 1) * LANES)
    total = weight_ref[stream, 0:1, lanes] * rows_ref[half, 8 + start : 16 + start, :]
    for j in range(1, weight_ref.shape[1]):
        moved = rows_ref[half, 8 + start - j : 16 + start - j, :]
        total = total + weight_ref[stream, j : j + 1, lanes] * moved
    return total


def pack_kernel(
    key_hbm,
    value_hbm,
    filter_hbm,
    weight_hbm,
    out_hbm,
    key_ref,
    value_ref,
    filter_ref,
    weight_ref,
    out_ref,
    key_rows,
    value_rows,
    product,
    extra,
    in_sem,
    out_sem,
):
    rim = weight_ref.shape[1] - 1
    channels, width = key_ref.shape
    group = out_ref.shape[0] // 2
    owners = group // 17
    per = channels // (2 * owners)
    arrivals = [pltpu.make_async_copy(weight_hbm, weight_ref, in_sem.at[0])]
    for half in range(2):
        mine = pl.ds(half * LANES, LANES)
        for n, (source, target) in enumerate(((key_hbm, key_ref), (value_hbm, value_ref))):
            arrivals.append(
                pltpu.make_async_copy(
                    source.at[mine, :], target.at[mine, :], in_sem.at[1 + 4 * half + n]
                )
            )
        for h in range(2):
            arrivals.append(
                pltpu.make_async_copy(
                    filter_hbm.at[mine, pl.ds(h * LANES, LANES)],
                    filter_ref.at[h, mine, :],
                    in_sem.at[3 + 4 * half + h],
                )
            )
    for copy in arrivals:
        copy.start()
    edge = jnp.zeros((8, LANES), F32)
    row = lax.broadcasted_iota(jnp.int32, (8, LANES), 0)
    arrivals[0].wait()
    departures = []
    for half in range(2):
        mine = slice(half * LANES, (half + 1) * LANES)
        for n, (rows, source) in enumerate(((key_rows, key_ref), (value_rows, value_ref))):
            rows[half, :8, :] = edge
            rows[half, 8 + width :, :] = edge
            arrivals[1 + 4 * half + n].wait()
            for h in range(2):
                part = slice(h * LANES, (h + 1) * LANES)
                rows[half, 8 + h * LANES : 8 + (h + 1) * LANES, :] = source[mine, part].T
        for h in range(2):
            parts = []
            for t in range(h * LANES, (h + 1) * LANES, 8):
                key = causal_taps_at(key_rows, weight_ref, 1, half, t)
                value = causal_taps_at(value_rows, weight_ref, 2, half, t)
                if t == 0:
                    value_head = value
                    parts.append(jnp.where(row < rim, key, key * value))
                else:
                    parts.append(key * value)
            product[h, mine, :] = jnp.concatenate(parts, axis=0).T
        key_spill = causal_taps_at(key_rows, weight_ref, 1, half, width)
        value_spill = causal_taps_at(value_rows, weight_ref, 2, half, width)
        ends = jnp.concatenate(
            [value_head, key_spill, value_spill, jnp.zeros((LANES - 24, LANES), F32)], axis=0
        )
        extra[mine, :] = ends.T
        arrivals[3 + 4 * half].wait()
        arrivals[4 + 4 * half].wait()
        start = half * group
        line = extra[pl.ds(half * LANES, owners, stride=per), :]
        for c in range(per):
            own = pl.ds(half * LANES + c, owners, stride=per)
            if c:
                line = line + pltpu.roll(extra[own, :], 32 * c, 1)
            for h in range(2):
                r = start + h * 4 + c
                out_ref[pl.ds(r, owners, stride=17), :] = product[h, own, :]
                out_ref[pl.ds(8 + r, owners, stride=17), :] = filter_ref[h, own, :]
        out_ref[pl.ds(start + 16, owners, stride=17), :] = line
        copy = pltpu.make_async_copy(
            out_ref.at[pl.ds(start, group), :], out_hbm.at[pl.ds(start, group), :], out_sem.at[half]
        )
        copy.start()
        departures.append(copy)
    for copy in departures:
        copy.wait()


def query_kernel(query_ref, rim_ref, weight_ref, out_ref, query_rows):
    rim = rim_ref.shape[0]
    width = query_ref.shape[1]
    for half in range(2):
        mine = slice(half * LANES, (half + 1) * LANES)
        query_rows[half, 8 - rim : 8, :] = rim_ref[:, mine]
        for h in range(2):
            part = slice(h * LANES, (h + 1) * LANES)
            query_rows[half, 8 + h * LANES : 8 + (h + 1) * LANES, :] = query_ref[mine, part].T
        for h in range(2):
            parts = [
                causal_taps_at(query_rows, weight_ref, 0, half, t)
                for t in range(h * LANES, (h + 1) * LANES, 8)
            ]
            out_ref[mine, h * LANES : (h + 1) * LANES] = jnp.concatenate(parts, axis=0).T


def conv_kernel(
    skip_ref, in_ref, rows_in, rows_out, turn, dft_high, dft_low, out_ref, zh, zl, gated, spec
):
    shards = in_ref.shape[0] // 17
    per = skip_ref.shape[0]
    rim = 6
    width = 2 * LANES
    lane = lax.broadcasted_iota(jnp.int32, (shards, LANES), 1)
    block = lax.broadcasted_iota(jnp.int32, (shards, LANES), 0)
    line = in_ref[pl.ds(16, shards, stride=17), :]
    prior = jnp.where(block == 0, 0.0, pltpu.roll(line, 1, 0))
    for c in range(per):
        here = pltpu.roll(line, (LANES - 32 * c) % LANES, 1) if c else line
        key_spill = pltpu.roll(prior, LANES - 32 * c - 8, 1)
        value_spill = pltpu.roll(prior, LANES - 32 * c - 16, 1)
        first = in_ref[pl.ds(c, shards, stride=17), :]
        first = jnp.where(lane < rim, (first + key_spill) * (here + value_spill), first)
        gated[c] = jnp.concatenate([first, in_ref[pl.ds(4 + c, shards, stride=17), :]], axis=1)
        taken = jnp.concatenate(
            [in_ref[pl.ds(8 + h * 4 + c, shards, stride=17), :] for h in range(2)], axis=1
        )
        for a, signal in enumerate((gated[c], taken)):
            high, low = split(signal)
            both = jnp.dot(
                rows_in[...],
                jnp.concatenate([high, low, high], axis=0),
                preferred_element_type=F32,
            )
            cos_part, sin_part = both[:shards], both[shards:]
            rows = pl.ds((a * per + c) * shards, shards)
            high, low = split(cos_part * turn[0] - sin_part * turn[1])
            zh[0, rows, :] = high
            zl[0, rows, :] = low
            high, low = split(cos_part * turn[1] + sin_part * turn[0])
            zh[1, rows, :] = high
            zl[1, rows, :] = low

    def times(lhs_high, lhs_low, which):
        return (
            jnp.dot(lhs_high, dft_high[which], preferred_element_type=F32)
            + jnp.dot(lhs_low, dft_high[which], preferred_element_type=F32)
            + jnp.dot(lhs_high, dft_low[which], preferred_element_type=F32)
        )

    spec[0] = times(zh[0], zl[0], 0) + times(zh[1], zl[1], 2)
    spec[1] = times(zh[0], zl[0], 1) + times(zh[1], zl[1], 0)
    count = per * shards
    sig_r, sig_i = spec[0, :count], spec[1, :count]
    fil_r, fil_i = spec[0, count:], spec[1, count:]
    real_high, real_low = split(sig_r * fil_r - sig_i * fil_i)
    imag_high, imag_low = split(sig_r * fil_i + sig_i * fil_r)
    back_r = times(real_high, real_low, 0) + times(imag_high, imag_low, 1)
    back_i = times(imag_high, imag_low, 0) + times(real_high, real_low, 2)
    spec[0, :count] = back_r
    spec[1, :count] = back_i
    for c in range(per):
        rows = pl.ds(c * shards, shards)
        br, bi = spec[0, rows, :], spec[1, rows, :]
        high, low = split(
            jnp.concatenate([br * turn[0] + bi * turn[1], bi * turn[0] - br * turn[1]], axis=0)
        )
        result = jnp.dot(
            rows_out[...], jnp.concatenate([high, low, high], axis=0), preferred_element_type=F32
        )
        result = result + skip_ref[c] * gated[c]
        for h in range(2):
            out_ref[pl.ds(h * 4 + c, shards, stride=8), :] = result[:, h * LANES : (h + 1) * LANES]


def gate_kernel(query_ref, conv_ref, out_ref):
    for m in range(query_ref.shape[0] // 8):
        rows = slice(m * 8, m * 8 + 8)
        one, two = conv_ref[m * 16 : m * 16 + 8, :], conv_ref[m * 16 + 8 : m * 16 + 16, :]
        left = jnp.concatenate([one[:4], two[:4]], axis=0)
        right = jnp.concatenate([one[4:], two[4:]], axis=0)
        out_ref[rows, :LANES] = query_ref[rows, :LANES] * left
        out_ref[rows, LANES:] = query_ref[rows, LANES:] * right


def limit(mebibytes):
    return pltpu.CompilerParams(vmem_limit_bytes=mebibytes * 1024 * 1024)


def on_device(query_in, key_in, value_in, short_weight, long_filter, skip_weight):
    channels, width = query_in.shape
    rim = short_weight.shape[1] - 1
    shards = lax.axis_size("ctx")
    per = channels // shards
    rows = pltpu.VMEM((2, width + 16, LANES), F32)
    packed = pl.pallas_call(
        pack_kernel,
        out_shape=jax.ShapeDtypeStruct((shards * 17, LANES), F32),
        in_specs=[HBM] * 4,
        out_specs=HBM,
        scratch_shapes=[
            pltpu.VMEM((channels, width), F32),
            pltpu.VMEM((channels, width), F32),
            pltpu.VMEM((2, channels, LANES), F32),
            pltpu.VMEM(short_weight.shape, F32),
            pltpu.VMEM((shards * 17, LANES), F32),
            rows,
            rows,
            pltpu.VMEM((2, channels, LANES), F32),
            pltpu.VMEM((channels, LANES), F32),
            pltpu.SemaphoreType.DMA((9,)),
            pltpu.SemaphoreType.DMA((2,)),
        ],
        compiler_params=limit(60),
        name="pack",
    )(key_in, value_in, long_filter, short_weight)
    packed, query_in, short_weight = lax.optimization_barrier((packed, query_in, short_weight))
    moved = lax.all_to_all(
        packed.reshape(shards, 1, 17 * LANES), "ctx", split_axis=0, concat_axis=0, tiled=True
    ).reshape(shards * 17, LANES)
    before = lax.ppermute(
        query_in[:, width - rim :].T, "ctx", [(i, i + 1) for i in range(shards - 1)]
    )
    query = pl.pallas_call(
        query_kernel,
        out_shape=jax.ShapeDtypeStruct((channels, width), F32),
        in_specs=[VMEM] * 3,
        out_specs=VMEM,
        scratch_shapes=[rows],
        compiler_params=limit(8),
        name="query",
    )(query_in, before, short_weight)
    skip = lax.dynamic_slice(skip_weight, (lax.axis_index("ctx") * per,), (per,))
    moved, query = lax.optimization_barrier((moved, query))
    constants = [jnp.asarray(t) for t in tables(shards, width)]
    convolved = pl.pallas_call(
        conv_kernel,
        out_shape=jax.ShapeDtypeStruct((shards * 8, LANES), F32),
        in_specs=[SMEM] + [VMEM] * 6,
        out_specs=VMEM,
        scratch_shapes=[
            pltpu.VMEM((2, 2 * channels, width), BF16),
            pltpu.VMEM((2, 2 * channels, width), BF16),
            pltpu.VMEM((per, shards, width), F32),
            pltpu.VMEM((2, 2 * channels, width), F32),
        ],
        compiler_params=limit(16),
        name="conv",
    )(skip, moved, *constants)
    returned = lax.all_to_all(
        convolved.reshape(shards, 8, LANES), "ctx", split_axis=0, concat_axis=0, tiled=True
    ).reshape(shards * 8, LANES)
    return pl.pallas_call(
        gate_kernel,
        out_shape=jax.ShapeDtypeStruct((channels, width), F32),
        in_specs=[VMEM] * 2,
        out_specs=VMEM,
        compiler_params=limit(8),
        name="gate",
    )(query, returned)


def solution(mesh):
    return jax.shard_map(
        on_device,
        mesh=mesh,
        in_specs=(
            P("grp", "ctx"),
            P("grp", "ctx"),
            P("grp", "ctx"),
            P(None, None, "grp"),
            P("grp", "ctx"),
            P("grp"),
        ),
        out_specs=P("grp", "ctx"),
        check_vma=False,
    )
```

```python
import functools
import math

import jax
import jax.numpy as jnp
import ml_dtypes
import numpy as np
from jax import lax
from jax.experimental import pallas as pl
from jax.experimental.pallas import tpu as pltpu
from jax.sharding import PartitionSpec as P

LANES = 128
STEP = 128
F32 = jnp.float32
BF16 = jnp.bfloat16
VMEM = pl.BlockSpec(memory_space=pltpu.VMEM)
HBM = pl.BlockSpec(memory_space=pltpu.HBM)
SMEM = pl.BlockSpec(memory_space=pltpu.SMEM)


def halves(table):
    high = table.astype(ml_dtypes.bfloat16)
    low = (table - high.astype(np.float64)).astype(ml_dtypes.bfloat16)
    return high, low


def split(x):
    high = x.astype(BF16)
    return high, (x - high.astype(F32)).astype(BF16)


def tables(blocks, width):
    odd = 2 * np.arange(blocks) + 1
    angle = 2.0 * math.pi * (odd[:, None] * np.arange(blocks)[None, :] % (4 * blocks)) / (4 * blocks)
    high, low = halves(np.concatenate([np.cos(angle), np.sin(angle)], axis=0))
    rows_in = np.concatenate([high, high, low], axis=1)
    scale = 1.0 / (blocks * width)
    high, low = halves(np.concatenate([np.cos(angle), np.sin(angle)], axis=0).T * scale)
    rows_out = np.concatenate([high, high, low], axis=1)
    order = 4 * blocks * width
    turn = 2.0 * math.pi * (odd[:, None] * np.arange(width)[None, :] % order) / order
    half = width // 2
    index = np.arange(half)
    fold = 2.0 * math.pi * np.broadcast_to(index, (blocks, half)) / width
    phase = 2.0 * math.pi * (index[:, None] * index[None, :] % half) / half
    cos, sin = np.cos(phase), np.sin(phase)
    forward = np.block([[cos, sin], [-sin, cos]])
    high, low = halves(np.stack([forward, forward.T]))
    return (
        rows_in,
        rows_out,
        np.stack([np.cos(turn), np.sin(turn)]).astype(np.float32),
        np.stack([np.cos(fold), np.sin(fold)]).astype(np.float32),
        np.concatenate([high, high, low], axis=1),
    )


def causal_taps_at(rows_ref, weight_ref, stream, half, start):
    lanes = slice(half * LANES, (half + 1) * LANES)
    total = weight_ref[stream, 0:1, lanes] * rows_ref[half, 8 + start : 16 + start, :]
    for j in range(1, weight_ref.shape[1]):
        moved = rows_ref[half, 8 + start - j : 16 + start - j, :]
        total = total + weight_ref[stream, j : j + 1, lanes] * moved
    return total


def pack_kernel(
    key_hbm,
    value_hbm,
    filter_hbm,
    weight_hbm,
    out_hbm,
    key_ref,
    value_ref,
    filter_ref,
    weight_ref,
    out_ref,
    key_rows,
    value_rows,
    product,
    extra,
    in_sem,
    out_sem,
):
    rim = weight_ref.shape[1] - 1
    channels, width = key_ref.shape
    group = out_ref.shape[0] // 2
    owners = group // 17
    per = channels // (2 * owners)
    arrivals = [pltpu.make_async_copy(weight_hbm, weight_ref, in_sem.at[0])]
    for half in range(2):
        mine = pl.ds(half * LANES, LANES)
        for n, (source, target) in enumerate(((key_hbm, key_ref), (value_hbm, value_ref))):
            arrivals.append(
                pltpu.make_async_copy(
                    source.at[mine, :], target.at[mine, :], in_sem.at[1 + 4 * half + n]
                )
            )
        for h in range(2):
            arrivals.append(
                pltpu.make_async_copy(
                    filter_hbm.at[mine, pl.ds(h * LANES, LANES)],
                    filter_ref.at[h, mine, :],
                    in_sem.at[3 + 4 * half + h],
                )
            )
    for copy in arrivals:
        copy.start()
    edge = jnp.zeros((8, LANES), F32)
    row = lax.broadcasted_iota(jnp.int32, (8, LANES), 0)
    arrivals[0].wait()
    departures = []
    for half in range(2):
        mine = slice(half * LANES, (half + 1) * LANES)
        for n, (rows, source) in enumerate(((key_rows, key_ref), (value_rows, value_ref))):
            rows[half, :8, :] = edge
            rows[half, 8 + width :, :] = edge
            arrivals[1 + 4 * half + n].wait()
            for h in range(2):
                part = slice(h * LANES, (h + 1) * LANES)
                rows[half, 8 + h * LANES : 8 + (h + 1) * LANES, :] = source[mine, part].T
        for h in range(2):
            parts = []
            for t in range(h * LANES, (h + 1) * LANES, 8):
                key = causal_taps_at(key_rows, weight_ref, 1, half, t)
                value = causal_taps_at(value_rows, weight_ref, 2, half, t)
                if t == 0:
                    value_head = value
                    parts.append(jnp.where(row < rim, key, key * value))
                else:
                    parts.append(key * value)
            product[h, mine, :] = jnp.concatenate(parts, axis=0).T
        key_spill = causal_taps_at(key_rows, weight_ref, 1, half, width)
        value_spill = causal_taps_at(value_rows, weight_ref, 2, half, width)
        ends = jnp.concatenate(
            [value_head, key_spill, value_spill, jnp.zeros((LANES - 24, LANES), F32)], axis=0
        )
        extra[mine, :] = ends.T
        arrivals[3 + 4 * half].wait()
        arrivals[4 + 4 * half].wait()
        start = half * group
        line = extra[pl.ds(half * LANES, owners, stride=per), :]
        for c in range(per):
            own = pl.ds(half * LANES + c, owners, stride=per)
            if c:
                line = line + pltpu.roll(extra[own, :], 32 * c, 1)
            for h in range(2):
                r = start + h * 4 + c
                out_ref[pl.ds(r, owners, stride=17), :] = product[h, own, :]
                out_ref[pl.ds(8 + r, owners, stride=17), :] = filter_ref[h, own, :]
        out_ref[pl.ds(start + 16, owners, stride=17), :] = line
        copy = pltpu.make_async_copy(
            out_ref.at[pl.ds(start, group), :], out_hbm.at[pl.ds(start, group), :], out_sem.at[half]
        )
        copy.start()
        departures.append(copy)
    for copy in departures:
        copy.wait()


def query_kernel(query_ref, rim_ref, weight_ref, out_ref, query_rows):
    rim = rim_ref.shape[0]
    width = query_ref.shape[1]
    for half in range(2):
        mine = slice(half * LANES, (half + 1) * LANES)
        query_rows[half, 8 - rim : 8, :] = rim_ref[:, mine]
        for h in range(2):
            part = slice(h * LANES, (h + 1) * LANES)
            query_rows[half, 8 + h * LANES : 8 + (h + 1) * LANES, :] = query_ref[mine, part].T
        for h in range(2):
            parts = [
                causal_taps_at(query_rows, weight_ref, 0, half, t)
                for t in range(h * LANES, (h + 1) * LANES, 8)
            ]
            out_ref[mine, h * LANES : (h + 1) * LANES] = jnp.concatenate(parts, axis=0).T


def conv_kernel(
    rim, skip_ref, in_ref, rows_in, rows_out, turn, fold, dft, out_ref, gated, first_step, lhs, spec
):
    shards = in_ref.shape[0] // 17
    per = skip_ref.shape[0]
    lane = lax.broadcasted_iota(jnp.int32, (shards, LANES), 1)
    block = lax.broadcasted_iota(jnp.int32, (shards, LANES), 0)
    line = in_ref[pl.ds(16, shards, stride=17), :]
    prior = jnp.where(block == 0, 0.0, pltpu.roll(line, 1, 0))
    left, right = slice(0, LANES), slice(LANES, 2 * LANES)

    def triple(value):
        top, rest = split(value)
        return jnp.concatenate([top, rest, top], axis=0)

    def put(rows, part, value):
        top, rest = split(value)
        for n, term in enumerate((top, rest, top)):
            lhs[rows, pl.ds((2 * n + part) * LANES, LANES)] = term

    signals = []
    for c in range(per):
        here = pltpu.roll(line, (LANES - 32 * c) % LANES, 1) if c else line
        key_spill = pltpu.roll(prior, LANES - 32 * c - 8, 1)
        value_spill = pltpu.roll(prior, LANES - 32 * c - 16, 1)
        first = in_ref[pl.ds(c, shards, stride=17), :]
        first = jnp.where(lane < rim, (first + key_spill) * (here + value_spill), first)
        second = in_ref[pl.ds(4 + c, shards, stride=17), :]
        gated[c, :, left] = first
        gated[c, :, right] = second
        signals.append(jnp.concatenate([first, second], axis=1))
    for c in range(per):
        signals.append(
            jnp.concatenate(
                [in_ref[pl.ds(8 + h * 4 + c, shards, stride=17), :] for h in range(2)], axis=1
            )
        )
    for n, signal in enumerate(signals):
        first_step[n] = jnp.dot(rows_in[...], triple(signal), preferred_element_type=F32)
    count = 2 * per * shards
    for n in range(2 * per):
        a, c = divmod(n, per)
        cos_part, sin_part = first_step[n, :shards, :], first_step[n, shards:, :]
        real = cos_part * turn[0] - sin_part * turn[1]
        imag = cos_part * turn[1] + sin_part * turn[0]
        even = pl.ds(a * count + c * shards, shards)
        odd = pl.ds(a * count + (per + c) * shards, shards)
        put(even, 0, real[:, left] + real[:, right])
        put(even, 1, imag[:, left] + imag[:, right])
        real, imag = real[:, left] - real[:, right], imag[:, left] - imag[:, right]
        put(odd, 0, real * fold[0] - imag * fold[1])
        put(odd, 1, real * fold[1] + imag * fold[0])
    for r in range(0, 2 * count, STEP):
        spec[r : r + STEP] = jnp.dot(
            lhs[r : r + STEP], dft[0], preferred_element_type=F32
        )
    for n in range(2 * per):
        rows = pl.ds(n * shards, shards)
        twin = pl.ds(count + n * shards, shards)
        sig_r, sig_i = spec[rows, left], spec[rows, right]
        fil_r, fil_i = spec[twin, left], spec[twin, right]
        put(rows, 0, sig_r * fil_r - sig_i * fil_i)
        put(rows, 1, sig_r * fil_i + sig_i * fil_r)
    for r in range(0, count, STEP):
        spec[r : r + STEP] = jnp.dot(
            lhs[r : r + STEP], dft[1], preferred_element_type=F32
        )
    values = []
    for c in range(per):
        even = pl.ds(c * shards, shards)
        odd = pl.ds((per + c) * shards, shards)
        real, imag = spec[odd, left], spec[odd, right]
        turned_r = real * fold[0] + imag * fold[1]
        turned_i = imag * fold[0] - real * fold[1]
        real, imag = spec[even, left], spec[even, right]
        real = jnp.concatenate([real + turned_r, real - turned_r], axis=1)
        imag = jnp.concatenate([imag + turned_i, imag - turned_i], axis=1)
        values.append(
            triple(
                jnp.concatenate(
                    [real * turn[0] + imag * turn[1], imag * turn[0] - real * turn[1]], axis=0
                )
            )
        )
    for c in range(per):
        result = jnp.dot(rows_out[...], values[c], preferred_element_type=F32)
        result = result + skip_ref[c] * gated[c]
        out_ref[pl.ds(c, shards, stride=8), :] = result[:, left]
        out_ref[pl.ds(4 + c, shards, stride=8), :] = result[:, right]


def gate_kernel(query_ref, conv_ref, out_ref):
    for m in range(query_ref.shape[0] // 8):
        rows = slice(m * 8, m * 8 + 8)
        one, two = conv_ref[m * 16 : m * 16 + 8, :], conv_ref[m * 16 + 8 : m * 16 + 16, :]
        left = jnp.concatenate([one[:4], two[:4]], axis=0)
        right = jnp.concatenate([one[4:], two[4:]], axis=0)
        out_ref[rows, :LANES] = query_ref[rows, :LANES] * left
        out_ref[rows, LANES:] = query_ref[rows, LANES:] * right


def limit(mebibytes):
    return pltpu.CompilerParams(vmem_limit_bytes=mebibytes * 1024 * 1024)


def on_device(query_in, key_in, value_in, short_weight, long_filter, skip_weight):
    channels, width = query_in.shape
    rim = short_weight.shape[1] - 1
    shards = lax.axis_size("ctx")
    per = channels // shards
    rows = pltpu.VMEM((2, width + 16, LANES), F32)
    packed = pl.pallas_call(
        pack_kernel,
        out_shape=jax.ShapeDtypeStruct((shards * 17, LANES), F32),
        in_specs=[HBM] * 4,
        out_specs=HBM,
        scratch_shapes=[
            pltpu.VMEM((channels, width), F32),
            pltpu.VMEM((channels, width), F32),
            pltpu.VMEM((2, channels, LANES), F32),
            pltpu.VMEM(short_weight.shape, F32),
            pltpu.VMEM((shards * 17, LANES), F32),
            rows,
            rows,
            pltpu.VMEM((2, channels, LANES), F32),
            pltpu.VMEM((channels, LANES), F32),
            pltpu.SemaphoreType.DMA((9,)),
            pltpu.SemaphoreType.DMA((2,)),
        ],
        compiler_params=limit(60),
        name="pack",
    )(key_in, value_in, long_filter, short_weight)
    packed, query_in, short_weight = lax.optimization_barrier((packed, query_in, short_weight))
    moved = lax.all_to_all(
        packed.reshape(shards, 1, 17 * LANES), "ctx", split_axis=0, concat_axis=0, tiled=True
    ).reshape(shards * 17, LANES)
    before = lax.ppermute(
        query_in[:, width - rim :].T, "ctx", [(i, i + 1) for i in range(shards - 1)]
    )
    query = pl.pallas_call(
        query_kernel,
        out_shape=jax.ShapeDtypeStruct((channels, width), F32),
        in_specs=[VMEM] * 3,
        out_specs=VMEM,
        scratch_shapes=[rows],
        compiler_params=limit(8),
        name="query",
    )(query_in, before, short_weight)
    skip = lax.dynamic_slice(skip_weight, (lax.axis_index("ctx") * per,), (per,))
    moved, query = lax.optimization_barrier((moved, query))
    constants = [jnp.asarray(t) for t in tables(shards, width)]
    convolved = pl.pallas_call(
        functools.partial(conv_kernel, rim),
        out_shape=jax.ShapeDtypeStruct((shards * 8, LANES), F32),
        in_specs=[SMEM] + [VMEM] * 6,
        out_specs=VMEM,
        scratch_shapes=[
            pltpu.VMEM((per, shards, width), F32),
            pltpu.VMEM((2 * per, 2 * shards, width), F32),
            pltpu.VMEM((4 * channels, 3 * width), BF16),
            pltpu.VMEM((4 * channels, width), F32),
        ],
        compiler_params=limit(16),
        name="conv",
    )(skip, moved, *constants)
    returned = lax.all_to_all(
        convolved.reshape(shards, 8, LANES), "ctx", split_axis=0, concat_axis=0, tiled=True
    ).reshape(shards * 8, LANES)
    return pl.pallas_call(
        gate_kernel,
        out_shape=jax.ShapeDtypeStruct((channels, width), F32),
        in_specs=[VMEM] * 2,
        out_specs=VMEM,
        compiler_params=limit(8),
        name="gate",
    )(query, returned)


def solution(mesh):
    return jax.shard_map(
        on_device,
        mesh=mesh,
        in_specs=(
            P("grp", "ctx"),
            P("grp", "ctx"),
            P("grp", "ctx"),
            P(None, None, "grp"),
            P("grp", "ctx"),
            P("grp"),
        ),
        out_specs=P("grp", "ctx"),
        check_vma=False,
    )
```

```python
import functools
import math

import jax
import jax.numpy as jnp
import ml_dtypes
import numpy as np
from jax import lax
from jax.experimental import pallas as pl
from jax.experimental.pallas import tpu as pltpu
from jax.sharding import PartitionSpec as P

LANES = 128
STEP = 128
F32 = jnp.float32
BF16 = jnp.bfloat16
VMEM = pl.BlockSpec(memory_space=pltpu.VMEM)
HBM = pl.BlockSpec(memory_space=pltpu.HBM)


def halves(table):
    high = table.astype(ml_dtypes.bfloat16)
    low = (table - high.astype(np.float64)).astype(ml_dtypes.bfloat16)
    return high, low


def split(x):
    high = x.astype(BF16)
    return high, (x - high.astype(F32)).astype(BF16)


def tables(blocks, width):
    odd = 2 * np.arange(blocks) + 1
    angle = 2.0 * math.pi * (odd[:, None] * np.arange(blocks)[None, :] % (4 * blocks)) / (4 * blocks)
    high, low = halves(np.concatenate([np.cos(angle), np.sin(angle)], axis=0))
    rows_in = np.concatenate([high, high, low], axis=1)
    scale = 1.0 / (blocks * width)
    high, low = halves(np.concatenate([np.cos(angle), np.sin(angle)], axis=0).T * scale)
    rows_out = np.concatenate([high, high, low], axis=1)
    order = 4 * blocks * width
    turn = 2.0 * math.pi * (odd[:, None] * np.arange(width)[None, :] % order) / order
    half = width // 2
    index = np.arange(half)
    fold = 2.0 * math.pi * np.broadcast_to(index, (blocks, half)) / width
    phase = 2.0 * math.pi * (index[:, None] * index[None, :] % half) / half
    cos, sin = np.cos(phase), np.sin(phase)
    forward = np.block([[cos, sin], [-sin, cos]])
    high, low = halves(np.stack([forward, forward.T]))
    return (
        rows_in,
        rows_out,
        np.stack([np.cos(turn), np.sin(turn)]).astype(np.float32),
        np.stack([np.cos(fold), np.sin(fold)]).astype(np.float32),
        np.concatenate([high, high, low], axis=1),
    )


def causal_taps_at(rows_ref, weight_ref, stream, half, start):
    lanes = slice(half * LANES, (half + 1) * LANES)
    total = weight_ref[stream, 0:1, lanes] * rows_ref[half, 8 + start : 16 + start, :]
    for j in range(1, weight_ref.shape[1]):
        moved = rows_ref[half, 8 + start - j : 16 + start - j, :]
        total = total + weight_ref[stream, j : j + 1, lanes] * moved
    return total


def pack_kernel(
    key_hbm,
    value_hbm,
    filter_hbm,
    weight_hbm,
    out_hbm,
    key_ref,
    value_ref,
    filter_ref,
    weight_ref,
    out_ref,
    key_rows,
    value_rows,
    product,
    extra,
    in_sem,
    out_sem,
):
    rim = weight_ref.shape[1] - 1
    channels, width = key_ref.shape
    group = out_ref.shape[0] // 2
    owners = group // 17
    per = channels // (2 * owners)
    arrivals = [pltpu.make_async_copy(weight_hbm, weight_ref, in_sem.at[0])]
    for half in range(2):
        mine = pl.ds(half * LANES, LANES)
        for n, (source, target) in enumerate(((key_hbm, key_ref), (value_hbm, value_ref))):
            arrivals.append(
                pltpu.make_async_copy(
                    source.at[mine, :], target.at[mine, :], in_sem.at[1 + 4 * half + n]
                )
            )
        for h in range(2):
            arrivals.append(
                pltpu.make_async_copy(
                    filter_hbm.at[mine, pl.ds(h * LANES, LANES)],
                    filter_ref.at[h, mine, :],
                    in_sem.at[3 + 4 * half + h],
                )
            )
    for copy in arrivals:
        copy.start()
    edge = jnp.zeros((8, LANES), F32)
    row = lax.broadcasted_iota(jnp.int32, (8, LANES), 0)
    arrivals[0].wait()
    departures = []
    for half in range(2):
        mine = slice(half * LANES, (half + 1) * LANES)
        for n, (rows, source) in enumerate(((key_rows, key_ref), (value_rows, value_ref))):
            rows[half, :8, :] = edge
            rows[half, 8 + width :, :] = edge
            arrivals[1 + 4 * half + n].wait()
            for h in range(2):
                part = slice(h * LANES, (h + 1) * LANES)
                rows[half, 8 + h * LANES : 8 + (h + 1) * LANES, :] = source[mine, part].T
        for h in range(2):
            parts = []
            for t in range(h * LANES, (h + 1) * LANES, 8):
                key = causal_taps_at(key_rows, weight_ref, 1, half, t)
                value = causal_taps_at(value_rows, weight_ref, 2, half, t)
                if t == 0:
                    value_head = value
                    parts.append(jnp.where(row < rim, key, key * value))
                else:
                    parts.append(key * value)
            product[h, mine, :] = jnp.concatenate(parts, axis=0).T
        key_spill = causal_taps_at(key_rows, weight_ref, 1, half, width)
        value_spill = causal_taps_at(value_rows, weight_ref, 2, half, width)
        ends = jnp.concatenate(
            [value_head, key_spill, value_spill, jnp.zeros((LANES - 24, LANES), F32)], axis=0
        )
        extra[mine, :] = ends.T
        arrivals[3 + 4 * half].wait()
        arrivals[4 + 4 * half].wait()
        start = half * group
        line = extra[pl.ds(half * LANES, owners, stride=per), :]
        for c in range(per):
            own = pl.ds(half * LANES + c, owners, stride=per)
            if c:
                line = line + pltpu.roll(extra[own, :], 32 * c, 1)
            for h in range(2):
                r = start + h * 4 + c
                out_ref[pl.ds(r, owners, stride=17), :] = product[h, own, :]
                out_ref[pl.ds(8 + r, owners, stride=17), :] = filter_ref[h, own, :]
        out_ref[pl.ds(start + 16, owners, stride=17), :] = line
        copy = pltpu.make_async_copy(
            out_ref.at[pl.ds(start, group), :], out_hbm.at[pl.ds(start, group), :], out_sem.at[half]
        )
        copy.start()
        departures.append(copy)
    for copy in departures:
        copy.wait()


def query_kernel(query_ref, rim_ref, weight_ref, out_ref, query_rows):
    rim = rim_ref.shape[0]
    width = query_ref.shape[1]
    for half in range(2):
        mine = slice(half * LANES, (half + 1) * LANES)
        query_rows[half, 8 - rim : 8, :] = rim_ref[:, mine]
        for h in range(2):
            part = slice(h * LANES, (h + 1) * LANES)
            query_rows[half, 8 + h * LANES : 8 + (h + 1) * LANES, :] = query_ref[mine, part].T
        for h in range(2):
            parts = [
                causal_taps_at(query_rows, weight_ref, 0, half, t)
                for t in range(h * LANES, (h + 1) * LANES, 8)
            ]
            out_ref[mine, h * LANES : (h + 1) * LANES] = jnp.concatenate(parts, axis=0).T


def conv_kernel(
    rim, skip_ref, in_ref, rows_in, rows_out, turn, fold, dft, out_ref, gated, first_step, lhs, spec
):
    shards = in_ref.shape[0] // 17
    per = skip_ref.shape[0]
    lane = lax.broadcasted_iota(jnp.int32, (shards, LANES), 1)
    block = lax.broadcasted_iota(jnp.int32, (shards, LANES), 0)
    line = in_ref[pl.ds(16, shards, stride=17), :]
    prior = jnp.where(block == 0, 0.0, pltpu.roll(line, 1, 0))
    left, right = slice(0, LANES), slice(LANES, 2 * LANES)

    def triple(value):
        top, rest = split(value)
        return jnp.concatenate([top, rest, top], axis=0)

    def put(rows, part, value):
        top, rest = split(value)
        for n, term in enumerate((top, rest, top)):
            lhs[rows, pl.ds((2 * n + part) * LANES, LANES)] = term

    signals = []
    for c in range(per):
        here = pltpu.roll(line, (LANES - 32 * c) % LANES, 1) if c else line
        key_spill = pltpu.roll(prior, LANES - 32 * c - 8, 1)
        value_spill = pltpu.roll(prior, LANES - 32 * c - 16, 1)
        first = in_ref[pl.ds(c, shards, stride=17), :]
        first = jnp.where(lane < rim, (first + key_spill) * (here + value_spill), first)
        second = in_ref[pl.ds(4 + c, shards, stride=17), :]
        gated[c, :, left] = first
        gated[c, :, right] = second
        signals.append(jnp.concatenate([first, second], axis=1))
    for c in range(per):
        signals.append(
            jnp.concatenate(
                [in_ref[pl.ds(8 + h * 4 + c, shards, stride=17), :] for h in range(2)], axis=1
            )
        )
    for n, signal in enumerate(signals):
        first_step[n] = jnp.dot(rows_in[...], triple(signal), preferred_element_type=F32)
    count = 2 * per * shards
    for n in range(2 * per):
        a, c = divmod(n, per)
        cos_part, sin_part = first_step[n, :shards, :], first_step[n, shards:, :]
        real = cos_part * turn[0] - sin_part * turn[1]
        imag = cos_part * turn[1] + sin_part * turn[0]
        even = pl.ds(a * count + c * shards, shards)
        odd = pl.ds(a * count + (per + c) * shards, shards)
        put(even, 0, real[:, left] + real[:, right])
        put(even, 1, imag[:, left] + imag[:, right])
        real, imag = real[:, left] - real[:, right], imag[:, left] - imag[:, right]
        put(odd, 0, real * fold[0] - imag * fold[1])
        put(odd, 1, real * fold[1] + imag * fold[0])
    for r in range(0, 2 * count, STEP):
        spec[r : r + STEP] = jnp.dot(
            lhs[r : r + STEP], dft[0], preferred_element_type=F32
        )
    for n in range(2 * per):
        rows = pl.ds(n * shards, shards)
        twin = pl.ds(count + n * shards, shards)
        sig_r, sig_i = spec[rows, left], spec[rows, right]
        fil_r, fil_i = spec[twin, left], spec[twin, right]
        put(rows, 0, sig_r * fil_r - sig_i * fil_i)
        put(rows, 1, sig_r * fil_i + sig_i * fil_r)
    for r in range(0, count, STEP):
        spec[r : r + STEP] = jnp.dot(
            lhs[r : r + STEP], dft[1], preferred_element_type=F32
        )
    values = []
    for c in range(per):
        even = pl.ds(c * shards, shards)
        odd = pl.ds((per + c) * shards, shards)
        real, imag = spec[odd, left], spec[odd, right]
        turned_r = real * fold[0] + imag * fold[1]
        turned_i = imag * fold[0] - real * fold[1]
        real, imag = spec[even, left], spec[even, right]
        real = jnp.concatenate([real + turned_r, real - turned_r], axis=1)
        imag = jnp.concatenate([imag + turned_i, imag - turned_i], axis=1)
        values.append(
            triple(
                jnp.concatenate(
                    [real * turn[0] + imag * turn[1], imag * turn[0] - real * turn[1]], axis=0
                )
            )
        )
    for c in range(per):
        result = jnp.dot(rows_out[...], values[c], preferred_element_type=F32)
        skip = skip_ref[c : c + 1, :]
        out_ref[pl.ds(c, shards, stride=8), :] = result[:, left] + skip * gated[c, :, left]
        out_ref[pl.ds(4 + c, shards, stride=8), :] = result[:, right] + skip * gated[c, :, right]


def gate_kernel(query_ref, conv_ref, out_ref):
    for m in range(query_ref.shape[0] // 8):
        rows = slice(m * 8, m * 8 + 8)
        one, two = conv_ref[m * 16 : m * 16 + 8, :], conv_ref[m * 16 + 8 : m * 16 + 16, :]
        left = jnp.concatenate([one[:4], two[:4]], axis=0)
        right = jnp.concatenate([one[4:], two[4:]], axis=0)
        out_ref[rows, :LANES] = query_ref[rows, :LANES] * left
        out_ref[rows, LANES:] = query_ref[rows, LANES:] * right


def limit(mebibytes):
    return pltpu.CompilerParams(vmem_limit_bytes=mebibytes * 1024 * 1024)


def on_device(query_in, key_in, value_in, short_weight, long_filter, skip_weight):
    channels, width = query_in.shape
    rim = short_weight.shape[1] - 1
    shards = lax.axis_size("ctx")
    per = channels // shards
    rows = pltpu.VMEM((2, width + 16, LANES), F32)
    packed = pl.pallas_call(
        pack_kernel,
        out_shape=jax.ShapeDtypeStruct((shards * 17, LANES), F32),
        in_specs=[HBM] * 4,
        out_specs=HBM,
        scratch_shapes=[
            pltpu.VMEM((channels, width), F32),
            pltpu.VMEM((channels, width), F32),
            pltpu.VMEM((2, channels, LANES), F32),
            pltpu.VMEM(short_weight.shape, F32),
            pltpu.VMEM((shards * 17, LANES), F32),
            rows,
            rows,
            pltpu.VMEM((2, channels, LANES), F32),
            pltpu.VMEM((channels, LANES), F32),
            pltpu.SemaphoreType.DMA((9,)),
            pltpu.SemaphoreType.DMA((2,)),
        ],
        compiler_params=limit(60),
        name="pack",
    )(key_in, value_in, long_filter, short_weight)
    packed, query_in, short_weight = lax.optimization_barrier((packed, query_in, short_weight))
    moved = lax.all_to_all(
        packed.reshape(shards, 1, 17 * LANES), "ctx", split_axis=0, concat_axis=0, tiled=True
    ).reshape(shards * 17, LANES)
    before = lax.ppermute(
        query_in[:, width - rim :].T, "ctx", [(i, i + 1) for i in range(shards - 1)]
    )
    query = pl.pallas_call(
        query_kernel,
        out_shape=jax.ShapeDtypeStruct((channels, width), F32),
        in_specs=[VMEM] * 3,
        out_specs=VMEM,
        scratch_shapes=[rows],
        compiler_params=limit(8),
        name="query",
    )(query_in, before, short_weight)
    skip = lax.dynamic_slice(skip_weight, (lax.axis_index("ctx") * per,), (per,))
    skip = jnp.broadcast_to(skip[:, None], (per, LANES))
    moved, query, skip = lax.optimization_barrier((moved, query, skip))
    constants = [jnp.asarray(t) for t in tables(shards, width)]
    convolved = pl.pallas_call(
        functools.partial(conv_kernel, rim),
        out_shape=jax.ShapeDtypeStruct((shards * 8, LANES), F32),
        in_specs=[VMEM] * 7,
        out_specs=VMEM,
        scratch_shapes=[
            pltpu.VMEM((per, shards, width), F32),
            pltpu.VMEM((2 * per, 2 * shards, width), F32),
            pltpu.VMEM((4 * channels, 3 * width), BF16),
            pltpu.VMEM((4 * channels, width), F32),
        ],
        compiler_params=limit(16),
        name="conv",
    )(skip, moved, *constants)
    returned = lax.all_to_all(
        convolved.reshape(shards, 8, LANES), "ctx", split_axis=0, concat_axis=0, tiled=True
    ).reshape(shards * 8, LANES)
    return pl.pallas_call(
        gate_kernel,
        out_shape=jax.ShapeDtypeStruct((channels, width), F32),
        in_specs=[VMEM] * 2,
        out_specs=VMEM,
        compiler_params=limit(8),
        name="gate",
    )(query, returned)


def solution(mesh):
    return jax.shard_map(
        on_device,
        mesh=mesh,
        in_specs=(
            P("grp", "ctx"),
            P("grp", "ctx"),
            P("grp", "ctx"),
            P(None, None, "grp"),
            P("grp", "ctx"),
            P("grp"),
        ),
        out_specs=P("grp", "ctx"),
        check_vma=False,
    )
```

```python
import functools
import math
import random

import jax
import jax.numpy as jnp
import ml_dtypes
import numpy as np
from jax import lax
from jax.experimental import pallas as pl
from jax.experimental.pallas import tpu as pltpu
from jax.sharding import PartitionSpec as P

LANES = 128
STEP = 128
F32 = jnp.float32
BF16 = jnp.bfloat16
VMEM = pl.BlockSpec(memory_space=pltpu.VMEM)
HBM = pl.BlockSpec(memory_space=pltpu.HBM)


def halves(table):
    high = table.astype(ml_dtypes.bfloat16)
    low = (table - high.astype(np.float64)).astype(ml_dtypes.bfloat16)
    return high, low


def peer_order(count):
    order = list(range(count))
    random.Random(1).shuffle(order)
    return order


def split(x):
    high = x.astype(BF16)
    return high, (x - high.astype(F32)).astype(BF16)


def tables(blocks, width, order):
    odd = 2 * np.arange(blocks) + 1
    angle = 2.0 * math.pi * (odd[:, None] * np.arange(blocks)[None, :] % (4 * blocks)) / (4 * blocks)
    arriving = angle[:, order]
    high, low = halves(np.concatenate([np.cos(arriving), np.sin(arriving)], axis=0))
    rows_in = np.concatenate([high, high, low], axis=1)
    scale = 1.0 / (blocks * width)
    high, low = halves(np.concatenate([np.cos(arriving), np.sin(arriving)], axis=0).T * scale)
    rows_out = np.concatenate([high, high, low], axis=1)
    order = 4 * blocks * width
    turn = 2.0 * math.pi * (odd[:, None] * np.arange(width)[None, :] % order) / order
    half = width // 2
    index = np.arange(half)
    fold = 2.0 * math.pi * np.broadcast_to(index, (blocks, half)) / width
    phase = 2.0 * math.pi * (index[:, None] * index[None, :] % half) / half
    cos, sin = np.cos(phase), np.sin(phase)
    forward = np.block([[cos, sin], [-sin, cos]])
    high, low = halves(np.stack([forward, forward.T]))
    return (
        rows_in,
        rows_out,
        np.stack([np.cos(turn), np.sin(turn)]).astype(np.float32),
        np.stack([np.cos(fold), np.sin(fold)]).astype(np.float32),
        np.concatenate([high, high, low], axis=1),
    )


def causal_taps_at(rows_ref, weight_ref, stream, half, start):
    lanes = slice(half * LANES, (half + 1) * LANES)
    total = weight_ref[stream, 0:1, lanes] * rows_ref[half, 8 + start : 16 + start, :]
    for j in range(1, weight_ref.shape[1]):
        moved = rows_ref[half, 8 + start - j : 16 + start - j, :]
        total = total + weight_ref[stream, j : j + 1, lanes] * moved
    return total


def pack_kernel(
    key_hbm,
    value_hbm,
    filter_hbm,
    weight_hbm,
    out_hbm,
    key_ref,
    value_ref,
    filter_ref,
    weight_ref,
    out_ref,
    key_rows,
    value_rows,
    product,
    extra,
    in_sem,
    out_sem,
):
    rim = weight_ref.shape[1] - 1
    channels, width = key_ref.shape
    group = out_ref.shape[0] // 2
    owners = group // 17
    per = channels // (2 * owners)
    arrivals = [pltpu.make_async_copy(weight_hbm, weight_ref, in_sem.at[0])]
    for half in range(2):
        mine = pl.ds(half * LANES, LANES)
        for n, (source, target) in enumerate(((key_hbm, key_ref), (value_hbm, value_ref))):
            arrivals.append(
                pltpu.make_async_copy(
                    source.at[mine, :], target.at[mine, :], in_sem.at[1 + 4 * half + n]
                )
            )
        for h in range(2):
            arrivals.append(
                pltpu.make_async_copy(
                    filter_hbm.at[mine, pl.ds(h * LANES, LANES)],
                    filter_ref.at[h, mine, :],
                    in_sem.at[3 + 4 * half + h],
                )
            )
    for copy in arrivals:
        copy.start()
    edge = jnp.zeros((8, LANES), F32)
    row = lax.broadcasted_iota(jnp.int32, (8, LANES), 0)
    arrivals[0].wait()
    departures = []
    for half in range(2):
        mine = slice(half * LANES, (half + 1) * LANES)
        for n, (rows, source) in enumerate(((key_rows, key_ref), (value_rows, value_ref))):
            rows[half, :8, :] = edge
            rows[half, 8 + width :, :] = edge
            arrivals[1 + 4 * half + n].wait()
            for h in range(2):
                part = slice(h * LANES, (h + 1) * LANES)
                rows[half, 8 + h * LANES : 8 + (h + 1) * LANES, :] = source[mine, part].T
        for h in range(2):
            parts = []
            for t in range(h * LANES, (h + 1) * LANES, 8):
                key = causal_taps_at(key_rows, weight_ref, 1, half, t)
                value = causal_taps_at(value_rows, weight_ref, 2, half, t)
                if t == 0:
                    value_head = value
                    parts.append(jnp.where(row < rim, key, key * value))
                else:
                    parts.append(key * value)
            product[h, mine, :] = jnp.concatenate(parts, axis=0).T
        key_spill = causal_taps_at(key_rows, weight_ref, 1, half, width)
        value_spill = causal_taps_at(value_rows, weight_ref, 2, half, width)
        ends = jnp.concatenate(
            [value_head, key_spill, value_spill, jnp.zeros((LANES - 24, LANES), F32)], axis=0
        )
        extra[mine, :] = ends.T
        arrivals[3 + 4 * half].wait()
        arrivals[4 + 4 * half].wait()
        start = half * group
        line = extra[pl.ds(half * LANES, owners, stride=per), :]
        for c in range(per):
            own = pl.ds(half * LANES + c, owners, stride=per)
            if c:
                line = line + pltpu.roll(extra[own, :], 32 * c, 1)
            for h in range(2):
                r = start + h * 4 + c
                out_ref[pl.ds(r, owners, stride=17), :] = product[h, own, :]
                out_ref[pl.ds(8 + r, owners, stride=17), :] = filter_ref[h, own, :]
        out_ref[pl.ds(start + 16, owners, stride=17), :] = line
        copy = pltpu.make_async_copy(
            out_ref.at[pl.ds(start, group), :], out_hbm.at[pl.ds(start, group), :], out_sem.at[half]
        )
        copy.start()
        departures.append(copy)
    for copy in departures:
        copy.wait()


def query_kernel(query_ref, rim_ref, weight_ref, out_ref, query_rows):
    rim = rim_ref.shape[0]
    width = query_ref.shape[1]
    for half in range(2):
        mine = slice(half * LANES, (half + 1) * LANES)
        query_rows[half, 8 - rim : 8, :] = rim_ref[:, mine]
        for h in range(2):
            part = slice(h * LANES, (h + 1) * LANES)
            query_rows[half, 8 + h * LANES : 8 + (h + 1) * LANES, :] = query_ref[mine, part].T
        for h in range(2):
            parts = [
                causal_taps_at(query_rows, weight_ref, 0, half, t)
                for t in range(h * LANES, (h + 1) * LANES, 8)
            ]
            out_ref[mine, h * LANES : (h + 1) * LANES] = jnp.concatenate(parts, axis=0).T


def conv_kernel(
    rim, order, skip_ref, in_ref, rows_in, rows_out, turn, fold, dft, out_ref, prior_ref, first_step, lhs, spec
):
    shards = in_ref.shape[0] // 17
    per = skip_ref.shape[0]
    lane = lax.broadcasted_iota(jnp.int32, (shards, LANES), 1)
    block = lax.broadcasted_iota(jnp.int32, (shards, LANES), 0)
    line = in_ref[pl.ds(16, shards, stride=17), :]
    for r, here in enumerate(order):
        if here == 0:
            start = r
            prior_ref[r : r + 1, :] = jnp.zeros((1, LANES), F32)
        else:
            before = 17 * order.index(here - 1) + 16
            prior_ref[r : r + 1, :] = in_ref[before : before + 1, :]
    prior = prior_ref[...]
    zero_lag = (block == start) & (lane == 0)
    left, right = slice(0, LANES), slice(LANES, 2 * LANES)

    def triple(value):
        top, rest = split(value)
        return jnp.concatenate([top, rest, top], axis=0)

    def put(rows, part, value):
        top, rest = split(value)
        for n, term in enumerate((top, rest, top)):
            lhs[rows, pl.ds((2 * n + part) * LANES, LANES)] = term

    signals = []
    for c in range(per):
        here = pltpu.roll(line, (LANES - 32 * c) % LANES, 1) if c else line
        key_spill = pltpu.roll(prior, LANES - 32 * c - 8, 1)
        value_spill = pltpu.roll(prior, LANES - 32 * c - 16, 1)
        first = in_ref[pl.ds(c, shards, stride=17), :]
        first = jnp.where(lane < rim, (first + key_spill) * (here + value_spill), first)
        second = in_ref[pl.ds(4 + c, shards, stride=17), :]
        signals.append(jnp.concatenate([first, second], axis=1))
    for c in range(per):
        first = in_ref[pl.ds(8 + c, shards, stride=17), :]
        first = first + jnp.where(zero_lag, skip_ref[c : c + 1, :], 0.0)
        second = in_ref[pl.ds(12 + c, shards, stride=17), :]
        signals.append(jnp.concatenate([first, second], axis=1))
    for n, signal in enumerate(signals):
        first_step[n] = jnp.dot(rows_in[...], triple(signal), preferred_element_type=F32)
    count = 2 * per * shards
    for n in range(2 * per):
        a, c = divmod(n, per)
        cos_part, sin_part = first_step[n, :shards, :], first_step[n, shards:, :]
        real = cos_part * turn[0] - sin_part * turn[1]
        imag = cos_part * turn[1] + sin_part * turn[0]
        even = pl.ds(a * count + c * shards, shards)
        odd = pl.ds(a * count + (per + c) * shards, shards)
        put(even, 0, real[:, left] + real[:, right])
        put(even, 1, imag[:, left] + imag[:, right])
        real, imag = real[:, left] - real[:, right], imag[:, left] - imag[:, right]
        put(odd, 0, real * fold[0] - imag * fold[1])
        put(odd, 1, real * fold[1] + imag * fold[0])
    for r in range(0, 2 * count, STEP):
        spec[r : r + STEP] = jnp.dot(
            lhs[r : r + STEP], dft[0], preferred_element_type=F32
        )
    for n in range(2 * per):
        rows = pl.ds(n * shards, shards)
        twin = pl.ds(count + n * shards, shards)
        sig_r, sig_i = spec[rows, left], spec[rows, right]
        fil_r, fil_i = spec[twin, left], spec[twin, right]
        put(rows, 0, sig_r * fil_r - sig_i * fil_i)
        put(rows, 1, sig_r * fil_i + sig_i * fil_r)
    for r in range(0, count, STEP):
        spec[r : r + STEP] = jnp.dot(
            lhs[r : r + STEP], dft[1], preferred_element_type=F32
        )
    values = []
    for c in range(per):
        even = pl.ds(c * shards, shards)
        odd = pl.ds((per + c) * shards, shards)
        real, imag = spec[odd, left], spec[odd, right]
        turned_r = real * fold[0] + imag * fold[1]
        turned_i = imag * fold[0] - real * fold[1]
        real, imag = spec[even, left], spec[even, right]
        real = jnp.concatenate([real + turned_r, real - turned_r], axis=1)
        imag = jnp.concatenate([imag + turned_i, imag - turned_i], axis=1)
        values.append(
            triple(
                jnp.concatenate(
                    [real * turn[0] + imag * turn[1], imag * turn[0] - real * turn[1]], axis=0
                )
            )
        )
    for c in range(per):
        result = jnp.dot(rows_out[...], values[c], preferred_element_type=F32)
        out_ref[pl.ds(c, shards, stride=8), :] = result[:, left]
        out_ref[pl.ds(4 + c, shards, stride=8), :] = result[:, right]


def gate_kernel(query_ref, conv_ref, out_ref):
    for m in range(query_ref.shape[0] // 8):
        rows = slice(m * 8, m * 8 + 8)
        one, two = conv_ref[m * 16 : m * 16 + 8, :], conv_ref[m * 16 + 8 : m * 16 + 16, :]
        left = jnp.concatenate([one[:4], two[:4]], axis=0)
        right = jnp.concatenate([one[4:], two[4:]], axis=0)
        out_ref[rows, :LANES] = query_ref[rows, :LANES] * left
        out_ref[rows, LANES:] = query_ref[rows, LANES:] * right


def limit(mebibytes):
    return pltpu.CompilerParams(vmem_limit_bytes=mebibytes * 1024 * 1024)


def on_device(query_in, key_in, value_in, short_weight, long_filter, skip_weight):
    channels, width = query_in.shape
    rim = short_weight.shape[1] - 1
    shards = lax.axis_size("ctx")
    per = channels // shards
    order = peer_order(shards)
    rows = pltpu.VMEM((2, width + 16, LANES), F32)
    packed = pl.pallas_call(
        pack_kernel,
        out_shape=jax.ShapeDtypeStruct((shards * 17, LANES), F32),
        in_specs=[HBM] * 4,
        out_specs=HBM,
        scratch_shapes=[
            pltpu.VMEM((channels, width), F32),
            pltpu.VMEM((channels, width), F32),
            pltpu.VMEM((2, channels, LANES), F32),
            pltpu.VMEM(short_weight.shape, F32),
            pltpu.VMEM((shards * 17, LANES), F32),
            rows,
            rows,
            pltpu.VMEM((2, channels, LANES), F32),
            pltpu.VMEM((channels, LANES), F32),
            pltpu.SemaphoreType.DMA((9,)),
            pltpu.SemaphoreType.DMA((2,)),
        ],
        compiler_params=limit(60),
        name="pack",
    )(key_in, value_in, long_filter, short_weight)
    packed, query_in, short_weight = lax.optimization_barrier((packed, query_in, short_weight))
    moved = lax.all_to_all(
        packed.reshape(shards, 1, 17 * LANES),
        "ctx",
        split_axis=0,
        concat_axis=0,
        axis_index_groups=[order],
        tiled=True,
    ).reshape(shards * 17, LANES)
    before = lax.ppermute(
        query_in[:, width - rim :].T, "ctx", [(i, i + 1) for i in range(shards - 1)]
    )
    query = pl.pallas_call(
        query_kernel,
        out_shape=jax.ShapeDtypeStruct((channels, width), F32),
        in_specs=[VMEM] * 3,
        out_specs=VMEM,
        scratch_shapes=[rows],
        compiler_params=limit(8),
        name="query",
    )(query_in, before, short_weight)
    rank = jnp.asarray(np.argsort(order), jnp.int32)[lax.axis_index("ctx")]
    skip = lax.dynamic_slice(skip_weight, (rank * per,), (per,))
    skip = jnp.broadcast_to(skip[:, None], (per, LANES))
    moved, query, skip = lax.optimization_barrier((moved, query, skip))
    constants = [jnp.asarray(t) for t in tables(shards, width, order)]
    convolved = pl.pallas_call(
        functools.partial(conv_kernel, rim, order),
        out_shape=jax.ShapeDtypeStruct((shards * 8, LANES), F32),
        in_specs=[VMEM] * 7,
        out_specs=VMEM,
        scratch_shapes=[
            pltpu.VMEM((shards, LANES), F32),
            pltpu.VMEM((2 * per, 2 * shards, width), F32),
            pltpu.VMEM((4 * channels, 3 * width), BF16),
            pltpu.VMEM((4 * channels, width), F32),
        ],
        compiler_params=limit(16),
        name="conv",
    )(skip, moved, *constants)
    returned = lax.all_to_all(
        convolved.reshape(shards, 8, LANES),
        "ctx",
        split_axis=0,
        concat_axis=0,
        axis_index_groups=[order],
        tiled=True,
    ).reshape(shards * 8, LANES)
    return pl.pallas_call(
        gate_kernel,
        out_shape=jax.ShapeDtypeStruct((channels, width), F32),
        in_specs=[VMEM] * 2,
        out_specs=VMEM,
        compiler_params=limit(8),
        name="gate",
    )(query, returned)


def solution(mesh):
    return jax.shard_map(
        on_device,
        mesh=mesh,
        in_specs=(
            P("grp", "ctx"),
            P("grp", "ctx"),
            P("grp", "ctx"),
            P(None, None, "grp"),
            P("grp", "ctx"),
            P("grp"),
        ),
        out_specs=P("grp", "ctx"),
        check_vma=False,
    )
```

```python
import functools
import math
import random

import jax
import jax.numpy as jnp
import ml_dtypes
import numpy as np
from jax import lax
from jax.experimental import pallas as pl
from jax.experimental.pallas import tpu as pltpu
from jax.sharding import PartitionSpec as P

LANES = 128
STEP = 128
F32 = jnp.float32
BF16 = jnp.bfloat16
VMEM = pl.BlockSpec(memory_space=pltpu.VMEM)
HBM = pl.BlockSpec(memory_space=pltpu.HBM)


def halves(table):
    high = table.astype(ml_dtypes.bfloat16)
    low = (table - high.astype(np.float64)).astype(ml_dtypes.bfloat16)
    return high, low


def peer_order(count):
    order = list(range(count))
    random.Random(21).shuffle(order)
    return order


def split(x):
    high = x.astype(BF16)
    return high, (x - high.astype(F32)).astype(BF16)


def tables(blocks, width, order):
    odd = 2 * np.arange(blocks) + 1
    angle = 2.0 * math.pi * (odd[:, None] * np.arange(blocks)[None, :] % (4 * blocks)) / (4 * blocks)
    arriving = angle[:, order]
    high, low = halves(np.concatenate([np.cos(arriving), np.sin(arriving)], axis=0))
    rows_in = np.concatenate([high, high, low], axis=1)
    scale = 1.0 / (blocks * width)
    high, low = halves(np.concatenate([np.cos(arriving), np.sin(arriving)], axis=0).T * scale)
    rows_out = np.concatenate([high, high, low], axis=1)
    order = 4 * blocks * width
    turn = 2.0 * math.pi * (odd[:, None] * np.arange(width)[None, :] % order) / order
    half = width // 2
    index = np.arange(half)
    fold = 2.0 * math.pi * np.broadcast_to(index, (blocks, half)) / width
    phase = 2.0 * math.pi * (index[:, None] * index[None, :] % half) / half
    cos, sin = np.cos(phase), np.sin(phase)
    forward = np.block([[cos, sin], [-sin, cos]])
    high, low = halves(np.stack([forward, forward.T]))
    return (
        rows_in,
        rows_out,
        np.stack([np.cos(turn), np.sin(turn)]).astype(np.float32),
        np.stack([np.cos(fold), np.sin(fold)]).astype(np.float32),
        np.concatenate([high, high, low], axis=1),
    )


def causal_taps_at(rows_ref, weight_ref, stream, half, start):
    lanes = slice(half * LANES, (half + 1) * LANES)
    total = weight_ref[stream, 0:1, lanes] * rows_ref[half, 8 + start : 16 + start, :]
    for j in range(1, weight_ref.shape[1]):
        moved = rows_ref[half, 8 + start - j : 16 + start - j, :]
        total = total + weight_ref[stream, j : j + 1, lanes] * moved
    return total


def pack_kernel(
    key_hbm,
    value_hbm,
    filter_hbm,
    weight_hbm,
    out_hbm,
    key_ref,
    value_ref,
    filter_ref,
    weight_ref,
    out_ref,
    key_rows,
    value_rows,
    product,
    extra,
    in_sem,
    out_sem,
):
    rim = weight_ref.shape[1] - 1
    channels, width = key_ref.shape
    group = out_ref.shape[0] // 2
    owners = group // 17
    per = channels // (2 * owners)
    arrivals = [pltpu.make_async_copy(weight_hbm, weight_ref, in_sem.at[0])]
    for half in range(2):
        mine = pl.ds(half * LANES, LANES)
        for n, (source, target) in enumerate(((key_hbm, key_ref), (value_hbm, value_ref))):
            arrivals.append(
                pltpu.make_async_copy(
                    source.at[mine, :], target.at[mine, :], in_sem.at[1 + 4 * half + n]
                )
            )
        for h in range(2):
            arrivals.append(
                pltpu.make_async_copy(
                    filter_hbm.at[mine, pl.ds(h * LANES, LANES)],
                    filter_ref.at[h, mine, :],
                    in_sem.at[3 + 4 * half + h],
                )
            )
    for copy in arrivals:
        copy.start()
    edge = jnp.zeros((8, LANES), F32)
    row = lax.broadcasted_iota(jnp.int32, (8, LANES), 0)
    arrivals[0].wait()
    departures = []
    for half in range(2):
        mine = slice(half * LANES, (half + 1) * LANES)
        for n, (rows, source) in enumerate(((key_rows, key_ref), (value_rows, value_ref))):
            rows[half, :8, :] = edge
            rows[half, 8 + width :, :] = edge
            arrivals[1 + 4 * half + n].wait()
            for h in range(2):
                part = slice(h * LANES, (h + 1) * LANES)
                rows[half, 8 + h * LANES : 8 + (h + 1) * LANES, :] = source[mine, part].T
        for h in range(2):
            parts = []
            for t in range(h * LANES, (h + 1) * LANES, 8):
                key = causal_taps_at(key_rows, weight_ref, 1, half, t)
                value = causal_taps_at(value_rows, weight_ref, 2, half, t)
                if t == 0:
                    value_head = value
                    parts.append(jnp.where(row < rim, key, key * value))
                else:
                    parts.append(key * value)
            product[h, mine, :] = jnp.concatenate(parts, axis=0).T
        key_spill = causal_taps_at(key_rows, weight_ref, 1, half, width)
        value_spill = causal_taps_at(value_rows, weight_ref, 2, half, width)
        ends = jnp.concatenate(
            [value_head, key_spill, value_spill, jnp.zeros((LANES - 24, LANES), F32)], axis=0
        )
        extra[mine, :] = ends.T
        arrivals[3 + 4 * half].wait()
        arrivals[4 + 4 * half].wait()
        start = half * group
        line = extra[pl.ds(half * LANES, owners, stride=per), :]
        for c in range(per):
            own = pl.ds(half * LANES + c, owners, stride=per)
            if c:
                line = line + pltpu.roll(extra[own, :], 32 * c, 1)
            for h in range(2):
                r = start + h * 4 + c
                out_ref[pl.ds(r, owners, stride=17), :] = product[h, own, :]
                out_ref[pl.ds(8 + r, owners, stride=17), :] = filter_ref[h, own, :]
        out_ref[pl.ds(start + 16, owners, stride=17), :] = line
        copy = pltpu.make_async_copy(
            out_ref.at[pl.ds(start, group), :], out_hbm.at[pl.ds(start, group), :], out_sem.at[half]
        )
        copy.start()
        departures.append(copy)
    for copy in departures:
        copy.wait()


def query_kernel(query_ref, rim_ref, weight_ref, out_ref, query_rows):
    rim = rim_ref.shape[0]
    width = query_ref.shape[1]
    for half in range(2):
        mine = slice(half * LANES, (half + 1) * LANES)
        query_rows[half, 8 - rim : 8, :] = rim_ref[:, mine]
        for h in range(2):
            part = slice(h * LANES, (h + 1) * LANES)
            query_rows[half, 8 + h * LANES : 8 + (h + 1) * LANES, :] = query_ref[mine, part].T
        for h in range(2):
            parts = [
                causal_taps_at(query_rows, weight_ref, 0, half, t)
                for t in range(h * LANES, (h + 1) * LANES, 8)
            ]
            out_ref[mine, h * LANES : (h + 1) * LANES] = jnp.concatenate(parts, axis=0).T


def conv_kernel(
    rim, order, skip_ref, in_ref, rows_in, rows_out, turn, fold, dft, out_ref, prior_ref, first_step, lhs, spec
):
    shards = in_ref.shape[0] // 17
    per = skip_ref.shape[0]
    lane = lax.broadcasted_iota(jnp.int32, (shards, LANES), 1)
    block = lax.broadcasted_iota(jnp.int32, (shards, LANES), 0)
    line = in_ref[pl.ds(16, shards, stride=17), :]
    for r, here in enumerate(order):
        if here == 0:
            start = r
            prior_ref[r : r + 1, :] = jnp.zeros((1, LANES), F32)
        else:
            before = 17 * order.index(here - 1) + 16
            prior_ref[r : r + 1, :] = in_ref[before : before + 1, :]
    prior = prior_ref[...]
    zero_lag = (block == start) & (lane == 0)
    left, right = slice(0, LANES), slice(LANES, 2 * LANES)

    def triple(value):
        top, rest = split(value)
        return jnp.concatenate([top, rest, top], axis=0)

    def put(rows, part, value):
        top, rest = split(value)
        for n, term in enumerate((top, rest, top)):
            lhs[rows, pl.ds((2 * n + part) * LANES, LANES)] = term

    signals = []
    for c in range(per):
        here = pltpu.roll(line, (LANES - 32 * c) % LANES, 1) if c else line
        key_spill = pltpu.roll(prior, LANES - 32 * c - 8, 1)
        value_spill = pltpu.roll(prior, LANES - 32 * c - 16, 1)
        first = in_ref[pl.ds(c, shards, stride=17), :]
        first = jnp.where(lane < rim, (first + key_spill) * (here + value_spill), first)
        second = in_ref[pl.ds(4 + c, shards, stride=17), :]
        signals.append(jnp.concatenate([first, second], axis=1))
    for c in range(per):
        first = in_ref[pl.ds(8 + c, shards, stride=17), :]
        first = first + jnp.where(zero_lag, skip_ref[c : c + 1, :], 0.0)
        second = in_ref[pl.ds(12 + c, shards, stride=17), :]
        signals.append(jnp.concatenate([first, second], axis=1))
    for n, signal in enumerate(signals):
        first_step[n] = jnp.dot(rows_in[...], triple(signal), preferred_element_type=F32)
    count = 2 * per * shards
    for n in range(2 * per):
        a, c = divmod(n, per)
        cos_part, sin_part = first_step[n, :shards, :], first_step[n, shards:, :]
        real = cos_part * turn[0] - sin_part * turn[1]
        imag = cos_part * turn[1] + sin_part * turn[0]
        even = pl.ds(a * count + c * shards, shards)
        odd = pl.ds(a * count + (per + c) * shards, shards)
        put(even, 0, real[:, left] + real[:, right])
        put(even, 1, imag[:, left] + imag[:, right])
        real, imag = real[:, left] - real[:, right], imag[:, left] - imag[:, right]
        put(odd, 0, real * fold[0] - imag * fold[1])
        put(odd, 1, real * fold[1] + imag * fold[0])
    for r in range(0, 2 * count, STEP):
        spec[r : r + STEP] = jnp.dot(
            lhs[r : r + STEP], dft[0], preferred_element_type=F32
        )
    for n in range(2 * per):
        rows = pl.ds(n * shards, shards)
        twin = pl.ds(count + n * shards, shards)
        sig_r, sig_i = spec[rows, left], spec[rows, right]
        fil_r, fil_i = spec[twin, left], spec[twin, right]
        put(rows, 0, sig_r * fil_r - sig_i * fil_i)
        put(rows, 1, sig_r * fil_i + sig_i * fil_r)
    for r in range(0, count, STEP):
        spec[r : r + STEP] = jnp.dot(
            lhs[r : r + STEP], dft[1], preferred_element_type=F32
        )
    values = []
    for c in range(per):
        even = pl.ds(c * shards, shards)
        odd = pl.ds((per + c) * shards, shards)
        real, imag = spec[odd, left], spec[odd, right]
        turned_r = real * fold[0] + imag * fold[1]
        turned_i = imag * fold[0] - real * fold[1]
        real, imag = spec[even, left], spec[even, right]
        real = jnp.concatenate([real + turned_r, real - turned_r], axis=1)
        imag = jnp.concatenate([imag + turned_i, imag - turned_i], axis=1)
        values.append(
            triple(
                jnp.concatenate(
                    [real * turn[0] + imag * turn[1], imag * turn[0] - real * turn[1]], axis=0
                )
            )
        )
    for c in range(per):
        result = jnp.dot(rows_out[...], values[c], preferred_element_type=F32)
        out_ref[pl.ds(c, shards, stride=8), :] = result[:, left]
        out_ref[pl.ds(4 + c, shards, stride=8), :] = result[:, right]


def gate_kernel(query_ref, conv_ref, out_ref):
    for m in range(query_ref.shape[0] // 8):
        rows = slice(m * 8, m * 8 + 8)
        one, two = conv_ref[m * 16 : m * 16 + 8, :], conv_ref[m * 16 + 8 : m * 16 + 16, :]
        left = jnp.concatenate([one[:4], two[:4]], axis=0)
        right = jnp.concatenate([one[4:], two[4:]], axis=0)
        out_ref[rows, :LANES] = query_ref[rows, :LANES] * left
        out_ref[rows, LANES:] = query_ref[rows, LANES:] * right


def limit(mebibytes):
    return pltpu.CompilerParams(vmem_limit_bytes=mebibytes * 1024 * 1024)


def on_device(query_in, key_in, value_in, short_weight, long_filter, skip_weight):
    channels, width = query_in.shape
    rim = short_weight.shape[1] - 1
    shards = lax.axis_size("ctx")
    per = channels // shards
    order = peer_order(shards)
    rows = pltpu.VMEM((2, width + 16, LANES), F32)
    packed = pl.pallas_call(
        pack_kernel,
        out_shape=jax.ShapeDtypeStruct((shards * 17, LANES), F32),
        in_specs=[HBM] * 4,
        out_specs=HBM,
        scratch_shapes=[
            pltpu.VMEM((channels, width), F32),
            pltpu.VMEM((channels, width), F32),
            pltpu.VMEM((2, channels, LANES), F32),
            pltpu.VMEM(short_weight.shape, F32),
            pltpu.VMEM((shards * 17, LANES), F32),
            rows,
            rows,
            pltpu.VMEM((2, channels, LANES), F32),
            pltpu.VMEM((channels, LANES), F32),
            pltpu.SemaphoreType.DMA((9,)),
            pltpu.SemaphoreType.DMA((2,)),
        ],
        compiler_params=limit(60),
        name="pack",
    )(key_in, value_in, long_filter, short_weight)
    packed, query_in, short_weight = lax.optimization_barrier((packed, query_in, short_weight))
    moved = lax.all_to_all(
        packed.reshape(shards, 1, 17 * LANES),
        "ctx",
        split_axis=0,
        concat_axis=0,
        axis_index_groups=[order],
        tiled=True,
    ).reshape(shards * 17, LANES)
    before = lax.ppermute(
        query_in[:, width - rim :].T, "ctx", [(i, i + 1) for i in range(shards - 1)]
    )
    query = pl.pallas_call(
        query_kernel,
        out_shape=jax.ShapeDtypeStruct((channels, width), F32),
        in_specs=[VMEM] * 3,
        out_specs=VMEM,
        scratch_shapes=[rows],
        compiler_params=limit(8),
        name="query",
    )(query_in, before, short_weight)
    rank = jnp.asarray(np.argsort(order), jnp.int32)[lax.axis_index("ctx")]
    skip = lax.dynamic_slice(skip_weight, (rank * per,), (per,))
    skip = jnp.broadcast_to(skip[:, None], (per, LANES))
    moved, query, skip = lax.optimization_barrier((moved, query, skip))
    constants = [jnp.asarray(t) for t in tables(shards, width, order)]
    convolved = pl.pallas_call(
        functools.partial(conv_kernel, rim, order),
        out_shape=jax.ShapeDtypeStruct((shards * 8, LANES), F32),
        in_specs=[VMEM] * 7,
        out_specs=VMEM,
        scratch_shapes=[
            pltpu.VMEM((shards, LANES), F32),
            pltpu.VMEM((2 * per, 2 * shards, width), F32),
            pltpu.VMEM((4 * channels, 3 * width), BF16),
            pltpu.VMEM((4 * channels, width), F32),
        ],
        compiler_params=limit(16),
        name="conv",
    )(skip, moved, *constants)
    returned = lax.all_to_all(
        convolved.reshape(shards, 8, LANES),
        "ctx",
        split_axis=0,
        concat_axis=0,
        axis_index_groups=[order],
        tiled=True,
    ).reshape(shards * 8, LANES)
    return pl.pallas_call(
        gate_kernel,
        out_shape=jax.ShapeDtypeStruct((channels, width), F32),
        in_specs=[VMEM] * 2,
        out_specs=VMEM,
        compiler_params=limit(8),
        name="gate",
    )(query, returned)


def solution(mesh):
    return jax.shard_map(
        on_device,
        mesh=mesh,
        in_specs=(
            P("grp", "ctx"),
            P("grp", "ctx"),
            P("grp", "ctx"),
            P(None, None, "grp"),
            P("grp", "ctx"),
            P("grp"),
        ),
        out_specs=P("grp", "ctx"),
        check_vma=False,
    )
```

```python
import functools
import math
import random

import jax
import jax.numpy as jnp
import ml_dtypes
import numpy as np
from jax import lax
from jax.experimental import pallas as pl
from jax.experimental.pallas import tpu as pltpu
from jax.sharding import PartitionSpec as P

LANES = 128
STEP = 128
F32 = jnp.float32
BF16 = jnp.bfloat16
VMEM = pl.BlockSpec(memory_space=pltpu.VMEM)
HBM = pl.BlockSpec(memory_space=pltpu.HBM)


def halves(table):
    high = table.astype(ml_dtypes.bfloat16)
    low = (table - high.astype(np.float64)).astype(ml_dtypes.bfloat16)
    return high, low


def peer_order(count):
    order = list(range(count))
    random.Random(16).shuffle(order)
    return order


def split(x):
    high = x.astype(BF16)
    return high, (x - high.astype(F32)).astype(BF16)


def tables(blocks, width, order):
    odd = 2 * np.arange(blocks) + 1
    angle = 2.0 * math.pi * (odd[:, None] * np.arange(blocks)[None, :] % (4 * blocks)) / (4 * blocks)
    arriving = angle[:, order]
    high, low = halves(np.concatenate([np.cos(arriving), np.sin(arriving)], axis=0))
    rows_in = np.concatenate([high, high, low], axis=1)
    scale = 1.0 / (blocks * width)
    high, low = halves(np.concatenate([np.cos(arriving), np.sin(arriving)], axis=0).T * scale)
    rows_out = np.concatenate([high, high, low], axis=1)
    order = 4 * blocks * width
    turn = 2.0 * math.pi * (odd[:, None] * np.arange(width)[None, :] % order) / order
    half = width // 2
    index = np.arange(half)
    fold = 2.0 * math.pi * np.broadcast_to(index, (blocks, half)) / width
    phase = 2.0 * math.pi * (index[:, None] * index[None, :] % half) / half
    cos, sin = np.cos(phase), np.sin(phase)
    forward = np.block([[cos, sin], [-sin, cos]])
    high, low = halves(np.stack([forward, forward.T]))
    return (
        rows_in,
        rows_out,
        np.stack([np.cos(turn), np.sin(turn)]).astype(np.float32),
        np.stack([np.cos(fold), np.sin(fold)]).astype(np.float32),
        np.concatenate([high, high, low], axis=1),
    )


def causal_taps_at(rows_ref, weight_ref, stream, half, start):
    lanes = slice(half * LANES, (half + 1) * LANES)
    total = weight_ref[stream, 0:1, lanes] * rows_ref[half, 8 + start : 16 + start, :]
    for j in range(1, weight_ref.shape[1]):
        moved = rows_ref[half, 8 + start - j : 16 + start - j, :]
        total = total + weight_ref[stream, j : j + 1, lanes] * moved
    return total


def pack_kernel(
    key_hbm,
    value_hbm,
    filter_hbm,
    weight_hbm,
    out_hbm,
    key_ref,
    value_ref,
    filter_ref,
    weight_ref,
    out_ref,
    key_rows,
    value_rows,
    product,
    extra,
    in_sem,
    out_sem,
):
    rim = weight_ref.shape[1] - 1
    channels, width = key_ref.shape
    group = out_ref.shape[0] // 2
    owners = group // 17
    per = channels // (2 * owners)
    arrivals = [pltpu.make_async_copy(weight_hbm, weight_ref, in_sem.at[0])]
    for half in range(2):
        mine = pl.ds(half * LANES, LANES)
        for n, (source, target) in enumerate(((key_hbm, key_ref), (value_hbm, value_ref))):
            arrivals.append(
                pltpu.make_async_copy(
                    source.at[mine, :], target.at[mine, :], in_sem.at[1 + 4 * half + n]
                )
            )
        for h in range(2):
            arrivals.append(
                pltpu.make_async_copy(
                    filter_hbm.at[mine, pl.ds(h * LANES, LANES)],
                    filter_ref.at[h, mine, :],
                    in_sem.at[3 + 4 * half + h],
                )
            )
    for copy in arrivals:
        copy.start()
    edge = jnp.zeros((8, LANES), F32)
    row = lax.broadcasted_iota(jnp.int32, (8, LANES), 0)
    arrivals[0].wait()
    departures = []
    for half in range(2):
        mine = slice(half * LANES, (half + 1) * LANES)
        for n, (rows, source) in enumerate(((key_rows, key_ref), (value_rows, value_ref))):
            rows[half, :8, :] = edge
            rows[half, 8 + width :, :] = edge
            arrivals[1 + 4 * half + n].wait()
            for h in range(2):
                part = slice(h * LANES, (h + 1) * LANES)
                rows[half, 8 + h * LANES : 8 + (h + 1) * LANES, :] = source[mine, part].T
        for h in range(2):
            parts = []
            for t in range(h * LANES, (h + 1) * LANES, 8):
                key = causal_taps_at(key_rows, weight_ref, 1, half, t)
                value = causal_taps_at(value_rows, weight_ref, 2, half, t)
                if t == 0:
                    value_head = value
                    parts.append(jnp.where(row < rim, key, key * value))
                else:
                    parts.append(key * value)
            product[h, mine, :] = jnp.concatenate(parts, axis=0).T
        key_spill = causal_taps_at(key_rows, weight_ref, 1, half, width)
        value_spill = causal_taps_at(value_rows, weight_ref, 2, half, width)
        ends = jnp.concatenate(
            [value_head, key_spill, value_spill, jnp.zeros((LANES - 24, LANES), F32)], axis=0
        )
        extra[mine, :] = ends.T
        arrivals[3 + 4 * half].wait()
        arrivals[4 + 4 * half].wait()
        start = half * group
        line = extra[pl.ds(half * LANES, owners, stride=per), :]
        for c in range(per):
            own = pl.ds(half * LANES + c, owners, stride=per)
            if c:
                line = line + pltpu.roll(extra[own, :], 32 * c, 1)
            for h in range(2):
                r = start + h * 4 + c
                out_ref[pl.ds(r, owners, stride=17), :] = product[h, own, :]
                out_ref[pl.ds(8 + r, owners, stride=17), :] = filter_ref[h, own, :]
        out_ref[pl.ds(start + 16, owners, stride=17), :] = line
        copy = pltpu.make_async_copy(
            out_ref.at[pl.ds(start, group), :], out_hbm.at[pl.ds(start, group), :], out_sem.at[half]
        )
        copy.start()
        departures.append(copy)
    for copy in departures:
        copy.wait()


def query_kernel(query_ref, rim_ref, weight_ref, out_ref, query_rows):
    rim = rim_ref.shape[0]
    width = query_ref.shape[1]
    for half in range(2):
        mine = slice(half * LANES, (half + 1) * LANES)
        query_rows[half, 8 - rim : 8, :] = rim_ref[:, mine]
        for h in range(2):
            part = slice(h * LANES, (h + 1) * LANES)
            query_rows[half, 8 + h * LANES : 8 + (h + 1) * LANES, :] = query_ref[mine, part].T
        for h in range(2):
            parts = [
                causal_taps_at(query_rows, weight_ref, 0, half, t)
                for t in range(h * LANES, (h + 1) * LANES, 8)
            ]
            out_ref[mine, h * LANES : (h + 1) * LANES] = jnp.concatenate(parts, axis=0).T


def conv_kernel(
    rim, order, skip_ref, in_ref, rows_in, rows_out, turn, fold, dft, out_ref, prior_ref, first_step, lhs, spec
):
    shards = in_ref.shape[0] // 17
    per = skip_ref.shape[0]
    lane = lax.broadcasted_iota(jnp.int32, (shards, LANES), 1)
    block = lax.broadcasted_iota(jnp.int32, (shards, LANES), 0)
    line = in_ref[pl.ds(16, shards, stride=17), :]
    for r, here in enumerate(order):
        if here == 0:
            start = r
            prior_ref[r : r + 1, :] = jnp.zeros((1, LANES), F32)
        else:
            before = 17 * order.index(here - 1) + 16
            prior_ref[r : r + 1, :] = in_ref[before : before + 1, :]
    prior = prior_ref[...]
    zero_lag = (block == start) & (lane == 0)
    left, right = slice(0, LANES), slice(LANES, 2 * LANES)

    def triple(value):
        top, rest = split(value)
        return jnp.concatenate([top, rest, top], axis=0)

    def put(rows, part, value):
        top, rest = split(value)
        for n, term in enumerate((top, rest, top)):
            lhs[rows, pl.ds((2 * n + part) * LANES, LANES)] = term

    signals = []
    for c in range(per):
        here = pltpu.roll(line, (LANES - 32 * c) % LANES, 1) if c else line
        key_spill = pltpu.roll(prior, LANES - 32 * c - 8, 1)
        value_spill = pltpu.roll(prior, LANES - 32 * c - 16, 1)
        first = in_ref[pl.ds(c, shards, stride=17), :]
        first = jnp.where(lane < rim, (first + key_spill) * (here + value_spill), first)
        second = in_ref[pl.ds(4 + c, shards, stride=17), :]
        signals.append(jnp.concatenate([first, second], axis=1))
    for c in range(per):
        first = in_ref[pl.ds(8 + c, shards, stride=17), :]
        first = first + jnp.where(zero_lag, skip_ref[c : c + 1, :], 0.0)
        second = in_ref[pl.ds(12 + c, shards, stride=17), :]
        signals.append(jnp.concatenate([first, second], axis=1))
    for n, signal in enumerate(signals):
        first_step[n] = jnp.dot(rows_in[...], triple(signal), preferred_element_type=F32)
    count = 2 * per * shards
    for n in range(2 * per):
        a, c = divmod(n, per)
        cos_part, sin_part = first_step[n, :shards, :], first_step[n, shards:, :]
        real = cos_part * turn[0] - sin_part * turn[1]
        imag = cos_part * turn[1] + sin_part * turn[0]
        even = pl.ds(a * count + c * shards, shards)
        odd = pl.ds(a * count + (per + c) * shards, shards)
        put(even, 0, real[:, left] + real[:, right])
        put(even, 1, imag[:, left] + imag[:, right])
        real, imag = real[:, left] - real[:, right], imag[:, left] - imag[:, right]
        put(odd, 0, real * fold[0] - imag * fold[1])
        put(odd, 1, real * fold[1] + imag * fold[0])
    for r in range(0, 2 * count, STEP):
        spec[r : r + STEP] = jnp.dot(
            lhs[r : r + STEP], dft[0], preferred_element_type=F32
        )
    for n in range(2 * per):
        rows = pl.ds(n * shards, shards)
        twin = pl.ds(count + n * shards, shards)
        sig_r, sig_i = spec[rows, left], spec[rows, right]
        fil_r, fil_i = spec[twin, left], spec[twin, right]
        put(rows, 0, sig_r * fil_r - sig_i * fil_i)
        put(rows, 1, sig_r * fil_i + sig_i * fil_r)
    for r in range(0, count, STEP):
        spec[r : r + STEP] = jnp.dot(
            lhs[r : r + STEP], dft[1], preferred_element_type=F32
        )
    values = []
    for c in range(per):
        even = pl.ds(c * shards, shards)
        odd = pl.ds((per + c) * shards, shards)
        real, imag = spec[odd, left], spec[odd, right]
        turned_r = real * fold[0] + imag * fold[1]
        turned_i = imag * fold[0] - real * fold[1]
        real, imag = spec[even, left], spec[even, right]
        real = jnp.concatenate([real + turned_r, real - turned_r], axis=1)
        imag = jnp.concatenate([imag + turned_i, imag - turned_i], axis=1)
        values.append(
            triple(
                jnp.concatenate(
                    [real * turn[0] + imag * turn[1], imag * turn[0] - real * turn[1]], axis=0
                )
            )
        )
    for c in range(per):
        result = jnp.dot(rows_out[...], values[c], preferred_element_type=F32)
        out_ref[pl.ds(c, shards, stride=8), :] = result[:, left]
        out_ref[pl.ds(4 + c, shards, stride=8), :] = result[:, right]


def gate_kernel(query_ref, conv_ref, out_ref):
    for m in range(query_ref.shape[0] // 8):
        rows = slice(m * 8, m * 8 + 8)
        one, two = conv_ref[m * 16 : m * 16 + 8, :], conv_ref[m * 16 + 8 : m * 16 + 16, :]
        left = jnp.concatenate([one[:4], two[:4]], axis=0)
        right = jnp.concatenate([one[4:], two[4:]], axis=0)
        out_ref[rows, :LANES] = query_ref[rows, :LANES] * left
        out_ref[rows, LANES:] = query_ref[rows, LANES:] * right


def limit(mebibytes):
    return pltpu.CompilerParams(vmem_limit_bytes=mebibytes * 1024 * 1024)


def on_device(query_in, key_in, value_in, short_weight, long_filter, skip_weight):
    channels, width = query_in.shape
    rim = short_weight.shape[1] - 1
    shards = lax.axis_size("ctx")
    per = channels // shards
    order = peer_order(shards)
    rows = pltpu.VMEM((2, width + 16, LANES), F32)
    packed = pl.pallas_call(
        pack_kernel,
        out_shape=jax.ShapeDtypeStruct((shards * 17, LANES), F32),
        in_specs=[HBM] * 4,
        out_specs=HBM,
        scratch_shapes=[
            pltpu.VMEM((channels, width), F32),
            pltpu.VMEM((channels, width), F32),
            pltpu.VMEM((2, channels, LANES), F32),
            pltpu.VMEM(short_weight.shape, F32),
            pltpu.VMEM((shards * 17, LANES), F32),
            rows,
            rows,
            pltpu.VMEM((2, channels, LANES), F32),
            pltpu.VMEM((channels, LANES), F32),
            pltpu.SemaphoreType.DMA((9,)),
            pltpu.SemaphoreType.DMA((2,)),
        ],
        compiler_params=limit(60),
        name="pack",
    )(key_in, value_in, long_filter, short_weight)
    packed, query_in, short_weight = lax.optimization_barrier((packed, query_in, short_weight))
    moved = lax.all_to_all(
        packed.reshape(shards, 1, 17 * LANES),
        "ctx",
        split_axis=0,
        concat_axis=0,
        axis_index_groups=[order],
        tiled=True,
    ).reshape(shards * 17, LANES)
    before = lax.ppermute(
        query_in[:, width - rim :].T, "ctx", [(i, i + 1) for i in range(shards - 1)]
    )
    query = pl.pallas_call(
        query_kernel,
        out_shape=jax.ShapeDtypeStruct((channels, width), F32),
        in_specs=[VMEM] * 3,
        out_specs=VMEM,
        scratch_shapes=[rows],
        compiler_params=limit(8),
        name="query",
    )(query_in, before, short_weight)
    rank = jnp.asarray(np.argsort(order), jnp.int32)[lax.axis_index("ctx")]
    skip = lax.dynamic_slice(skip_weight, (rank * per,), (per,))
    skip = jnp.broadcast_to(skip[:, None], (per, LANES))
    moved, query, skip = lax.optimization_barrier((moved, query, skip))
    constants = [jnp.asarray(t) for t in tables(shards, width, order)]
    convolved = pl.pallas_call(
        functools.partial(conv_kernel, rim, order),
        out_shape=jax.ShapeDtypeStruct((shards * 8, LANES), F32),
        in_specs=[VMEM] * 7,
        out_specs=VMEM,
        scratch_shapes=[
            pltpu.VMEM((shards, LANES), F32),
            pltpu.VMEM((2 * per, 2 * shards, width), F32),
            pltpu.VMEM((4 * channels, 3 * width), BF16),
            pltpu.VMEM((4 * channels, width), F32),
        ],
        compiler_params=limit(16),
        name="conv",
    )(skip, moved, *constants)
    returned = lax.all_to_all(
        convolved.reshape(shards, 8, LANES),
        "ctx",
        split_axis=0,
        concat_axis=0,
        axis_index_groups=[order],
        tiled=True,
    ).reshape(shards * 8, LANES)
    return pl.pallas_call(
        gate_kernel,
        out_shape=jax.ShapeDtypeStruct((channels, width), F32),
        in_specs=[VMEM] * 2,
        out_specs=VMEM,
        compiler_params=limit(8),
        name="gate",
    )(query, returned)


def solution(mesh):
    return jax.shard_map(
        on_device,
        mesh=mesh,
        in_specs=(
            P("grp", "ctx"),
            P("grp", "ctx"),
            P("grp", "ctx"),
            P(None, None, "grp"),
            P("grp", "ctx"),
            P("grp"),
        ),
        out_specs=P("grp", "ctx"),
        check_vma=False,
    )
```
